32 devices in a mesh: sx: 4 (over y, x), sy: 4 (over z), par: 2 (over core).
Axes of the slice: x: 2, y: 2, z: 4, core: 2. Of those that a mesh axis runs over, the one named last changes fastest.
Arguments:
- initial_state: float32 [64, 64, 64, 128], P('par', 'sx', 'sy'), may hold values from -6 to 6
- conductivity: float32 [64, 64, 64, 128], P('par', 'sx', 'sy'), may hold values from 0.1 to 1
- omega: bfloat16 [64, 64], replicated, may hold values from -0.75 to 0.75
- psi: bfloat16 [64, 64, 64, 128], P(None, 'sx', 'sy'), may hold values from -0.01171875 to 0.01171875
- range_prev: bfloat16 [64, 64, 64, 128], P('par', 'sx', 'sy'), may hold values from -3 to 3
- corange_prev: float32 [64, 64], P(None, 'par'), may hold values from -3 to 3
Outputs:
- final_state: float32 [64, 64, 64, 128], P('par', 'sx', 'sy')
- range_sketch: bfloat16 [64, 64, 64, 128], P('par', 'sx', 'sy')
- corange_sketch: float32 [64, 64], P(None, 'par')
The draws below stay inside these ranges and needn't reach their ends.
All inputs are finite; a program needn't handle non-finite values.
Results may differ from the reference program's by a relative error of at most 0.0033.
Values may be sent and summed in bfloat16 or wider, within the bound.
No kernel may reach another device: no remote copies, remote signals or barrier semaphores. Data moves between devices by JAX's collectives and lax.ppermute only.
A program may use at most 192 MiB of HBM per device.

```python
import math
import jax
import jax.numpy as jnp

CX = 16
CY = 16
NZ = 128
R = 64
STEPS = 4
NX = 64
NY = 64
S = 64


def steps_of(stream_key, shape, cuts, least, top_value):
    def one(position, blocks):
        steps = jax.random.uniform(jax.random.fold_in(jax.random.fold_in(stream_key, 6), position), (blocks,), jnp.float32, least / len(cuts), top_value / len(cuts))
        return jnp.repeat(jnp.exp(steps), shape[position] // blocks).reshape((-1,) + (1,) * (len(shape) - position - 1))

    gain = one(*cuts[0])
    for cut in cuts[1:]:
        gain = gain * one(*cut)
    return gain


def centred(rng, extent, width, most, split=(), held_as=jnp.bfloat16):
    values = jax.random.normal(rng, extent, jnp.float32) * width
    if len(split) > 0:
        values = steps_of(rng, extent, split, -0.22, 0.18) * values
    return jnp.clip(values, min=-most, max=most).astype(held_as)


def setup_inputs(seed: int = 0) -> dict:
    streams_of = jax.random.split(jax.random.key(seed), 7)
    initial_state = centred(streams_of[0], (S, NX, NY, NZ), 1.0, 6.0, ((0, 2), (1, 4), (2, 4)), jnp.float32)
    conductivity = jnp.clip(jnp.exp(math.log(1.0) - 2.3025851 * jax.random.uniform(streams_of[1], (S, NX, NY, NZ), jnp.float32) ** steps_of(streams_of[1], (S, NX, NY, NZ), ((0, 2), (1, 4), (2, 4)), -0.2, 0.2)), 0.1, 1.0)
    omega = centred(streams_of[2], (S, R), S ** -0.5, 0.75)
    psi = centred(streams_of[3], (R, NX, NY, NZ), (8 * CX * CY * NZ) ** -0.5, 0.01171875, ((1, 4), (2, 4)))
    range_prev = centred(streams_of[4], (R, NX, NY, NZ), 0.5, 3.0, ((0, 2), (1, 4), (2, 4)))
    corange_prev = centred(streams_of[5], (R, S), 0.5, 3.0, ((1, 2),), jnp.float32)
    return {"initial_state": initial_state, "conductivity": conductivity, "omega": omega, "psi": psi, "range_prev": range_prev, "corange_prev": corange_prev}


def advance(state, conduct):
    field = jnp.pad(state, ((0, 0), (1, 1), (1, 1), (1, 1)))
    kpad = jnp.pad(conduct, ((0, 0), (1, 1), (1, 1), (1, 1)))
    center = field[:, 1:-1, 1:-1, 1:-1]
    kcen = kpad[:, 1:-1, 1:-1, 1:-1]
    shifts = [(2, 1, 1), (0, 1, 1), (1, 2, 1), (1, 0, 1), (1, 1, 2), (1, 1, 0)]
    total = jnp.zeros_like(center)
    for a, b, c in shifts:
        unb = field[:, a:a + center.shape[1], b:b + center.shape[2], c:c + center.shape[3]]
        knb = kpad[:, a:a + center.shape[1], b:b + center.shape[2], c:c + center.shape[3]]
        total = total + 0.5 * (kcen + knb) * (unb - center)
    return center + 0.16 * total


def reference(initial_state, conductivity, omega, psi, range_prev, corange_prev):
    state = initial_state
    for step in range(STEPS):
        state = advance(state, conductivity)
    snapshot = state.astype(jnp.bfloat16).astype(jnp.float32)
    range_new = jnp.einsum("sxyz,sr->rxyz", snapshot, omega.astype(jnp.float32))
    range_sketch = (range_prev.astype(jnp.float32) + range_new).astype(jnp.bfloat16)
    corange_new = jnp.einsum("rxyz,sxyz->rs", psi.astype(jnp.float32), snapshot)
    corange_sketch = corange_prev + corange_new
    return state, range_sketch, corange_sketch
```

```python
import functools

import jax
import jax.numpy as jnp
from jax import lax
from jax.experimental import pallas as pl
from jax.experimental.pallas import tpu as pltpu
from jax.sharding import PartitionSpec as P

STEPS = 4
BF = jnp.bfloat16
F32 = jnp.float32
HALF = 0.16 * 0.5


def vmem_call(kernel, outs, name, limit=8 << 20, scratch=(), hbm_in=(), hbm_out=(), flops=0, nbytes=0):
    def call(*args):
        in_specs = []
        ready = []
        for i, arg in enumerate(args):
            if i in hbm_in:
                in_specs.append(pl.BlockSpec(memory_space=pl.ANY))
                ready.append(arg)
            else:
                in_specs.append(pl.BlockSpec(memory_space=pltpu.VMEM))
                ready.append(pltpu.with_memory_space_constraint(arg, pltpu.VMEM))
        out_shape = []
        out_specs = []
        for i, (shape, dtype) in enumerate(outs):
            if i in hbm_out:
                out_shape.append(jax.ShapeDtypeStruct(shape, dtype))
                out_specs.append(pl.BlockSpec(memory_space=pl.ANY))
            else:
                out_shape.append(pltpu.VMEM(shape, dtype))
                out_specs.append(pl.BlockSpec(memory_space=pltpu.VMEM))
        return pl.pallas_call(
            kernel,
            out_shape=out_shape,
            in_specs=in_specs,
            out_specs=out_specs,
            scratch_shapes=list(scratch),
            name=name,
            compiler_params=pltpu.CompilerParams(vmem_limit_bytes=limit),
            cost_estimate=pl.CostEstimate(flops=flops, bytes_accessed=nbytes, transcendentals=0),
        )(*ready)

    return call


def row_of(ref, s, x):
    return ref[s, pl.ds(x, 1), :]


def merged(u_ref, faces, s, x, row):
    if faces is None:
        return u_ref[s, x]
    fx0, fx1, fy0, fy1 = faces
    last = u_ref.shape[1] - 1
    if x == 0:
        return fx0[s]
    if x == last:
        return fx1[s]
    value = u_ref[s, x]
    value = jnp.where(row == 0, row_of(fy0, s, x), value)
    return jnp.where(row == u_ref.shape[2] - 1, row_of(fy1, s, x), value)


def step_body(u_ref, k_ref, faces, w_ref, wfx0, wfx1, wfy0, wfy1):
    samples, nx, ny, nz = u_ref.shape
    row = lax.broadcasted_iota(jnp.int32, (ny, nz), 0)
    lane = lax.broadcasted_iota(jnp.int32, (ny, nz), 1)
    y_open = row < ny - 1
    z_open = lane < nz - 1
    z_edge = (lane == 0) | (lane == nz - 1)

    def body(s, carry):
        u = merged(u_ref, faces, s, 0, row)
        k = k_ref[s, 0] * HALF
        flux_low = None
        for x in range(nx):
            total = u
            if x + 1 < nx:
                u_next = merged(u_ref, faces, s, x + 1, row)
                k_next = k_ref[s, x + 1] * HALF
                flux = (k + k_next) * (u_next - u)
                total = total + flux
            if flux_low is not None:
                total = total - flux_low
            fy = (k + pltpu.roll(k, ny - 1, 0)) * (pltpu.roll(u, ny - 1, 0) - u)
            fy = jnp.where(y_open, fy, 0.0)
            total = total + fy - pltpu.roll(fy, 1, 0)
            fz = (k + pltpu.roll(k, nz - 1, 1)) * (pltpu.roll(u, nz - 1, 1) - u)
            fz = jnp.where(z_open, fz, 0.0)
            total = total + fz - pltpu.roll(fz, 1, 1)
            total = total - jnp.where(z_edge, k * u, 0.0)
            w_ref[s, x] = total
            if x == 0:
                wfx0[s] = total
            if x == nx - 1:
                wfx1[s] = total
            wfy0[s, pl.ds(x, 1), :] = total[0:1]
            wfy1[s, pl.ds(x, 1), :] = total[ny - 1 : ny]
            if x + 1 < nx:
                u, k, flux_low = u_next, k_next, flux
        return carry

    lax.fori_loop(0, samples, body, 0)


def first_kernel(u_ref, k_ref, w_ref, wfx0, wfx1, wfy0, wfy1):
    step_body(u_ref, k_ref, None, w_ref, wfx0, wfx1, wfy0, wfy1)


def step_kernel(u_ref, k_ref, fx0, fx1, fy0, fy1, w_ref, wfx0, wfx1, wfy0, wfy1):
    step_body(u_ref, k_ref, (fx0, fx1, fy0, fy1), w_ref, wfx0, wfx1, wfy0, wfy1)


def final_kernel(w_ref, fx0, fx1, fy0, fy1, out_ref, snap_ref, buf, sem):
    samples, nx, ny, nz = w_ref.shape
    row = lax.broadcasted_iota(jnp.int32, (ny, nz), 0)

    def copy_of(s):
        return pltpu.make_async_copy(buf.at[s], out_ref.at[s], sem.at[s])

    def body(s, carry):
        for x in range(nx):
            value = merged(w_ref, (fx0, fx1, fy0, fy1), s, x, row)
            buf[s, x] = value
            snap_ref[s, x] = value.astype(BF)
        copy_of(s).start()
        return carry

    lax.fori_loop(0, samples, body, 0)

    def finish(s, carry):
        copy_of(s).wait()
        return carry

    lax.fori_loop(0, samples, finish, 0)


def columns(ref, x, width):
    samples, _, ny, nz = ref.shape
    parts = [ref[:, x + i].reshape(samples * ny, nz) for i in range(width)]
    return jnp.concatenate(parts, axis=1)


def range_kernel(w_own_ref, w_other_ref, own_ref, other_ref, prev_ref, out_ref):
    ranks, nx, ny, nz = prev_ref.shape
    for x in range(0, nx, 2):
        value = jnp.dot(w_own_ref[...], columns(own_ref, x, 2), preferred_element_type=F32)
        value += jnp.dot(w_other_ref[...], columns(other_ref, x, 2), preferred_element_type=F32)
        for i in range(2):
            part = value[:, i * nz : (i + 1) * nz].reshape(ranks, ny, nz)
            out_ref[:, x + i] = (part + prev_ref[:, x + i].astype(F32)).astype(BF)


def corange_kernel(psi_ref, snap_ref, out_ref, acc):
    ranks, nx, ny, nz = psi_ref.shape
    samples = snap_ref.shape[0]
    cols = samples * ny
    acc[...] = jnp.zeros_like(acc)
    for x in range(0, nx, 2):
        left = columns(psi_ref, x, 2)
        right = columns(snap_ref, x, 2)
        acc[...] += lax.dot_general(left, right, (((1,), (1,)), ((), ())), preferred_element_type=F32)
    row = lax.broadcasted_iota(jnp.int32, (ny, cols), 0)
    col = lax.broadcasted_iota(jnp.int32, (ny, cols), 1) % ny
    same = row == col
    fold = (
        lax.broadcasted_iota(jnp.int32, (cols, samples), 0) // ny
        == lax.broadcasted_iota(jnp.int32, (cols, samples), 1)
    ).astype(F32)
    picked = jnp.where(same[None], acc[...].reshape(ranks, ny, cols), 0.0).sum(1)
    out_ref[...] = jnp.dot(picked, fold, precision=lax.Precision.HIGHEST, preferred_element_type=F32)


def swap_pairs(count, parity, par):
    partner = {}
    for i in range(parity, count - 1, 2):
        partner[i] = i + 1
        partner[i + 1] = i
    pairs = []
    for i in range(count):
        for p in range(par):
            source = i * par + p
            if i in partner:
                pairs.append((source, partner[i] * par + p))
            else:
                pairs.append((source, i * par + (p + 1) % par))
    return pairs


def exchange(low, high, axis):
    count, par = lax.axis_size(axis), lax.axis_size("par")
    index = lax.axis_index(axis)
    odd = index % 2 == 1
    first = lax.ppermute(jnp.where(odd, low, high), (axis, "par"), swap_pairs(count, 0, par))
    second = lax.ppermute(jnp.where(odd, high, low), (axis, "par"), swap_pairs(count, 1, par))
    zero = jnp.zeros_like(first)
    below = jnp.where(index == 0, zero, jnp.where(odd, first, second))
    above = jnp.where(index == count - 1, zero, jnp.where(odd, second, first))
    return below, above


def add_fluxes(base, state, coefs, halos):
    dx0, dx1, dy0, dy1 = (c * (h.astype(F32) - u) for c, h, u in zip(coefs, halos, state))
    fx0, fx1, fy0, fy1 = base
    ny, nx = fx0.shape[1], fy0.shape[1]
    yrow = lax.broadcasted_iota(jnp.int32, fx0.shape, 1)
    xrow = lax.broadcasted_iota(jnp.int32, fy0.shape, 1)

    def at_ends(index, count, low, high):
        return jnp.where(index == 0, low, 0.0) + jnp.where(index == count - 1, high, 0.0)

    return (
        fx0 + dx0 + at_ends(yrow, ny, dy0[:, :1], dy1[:, :1]),
        fx1 + dx1 + at_ends(yrow, ny, dy0[:, -1:], dy1[:, -1:]),
        fy0 + dy0 + at_ends(xrow, nx, dx0[:, :1], dx1[:, :1]),
        fy1 + dy1 + at_ends(xrow, nx, dx0[:, -1:], dx1[:, -1:]),
    )


def faces_of(block):
    return block[:, 0], block[:, -1], block[:, :, 0], block[:, :, -1]


def spread(block, ny):
    rows, cols = block.shape
    up = (jnp.arange(rows * ny)[:, None] // ny == jnp.arange(rows)[None, :]).astype(BF)
    across = (jnp.arange(cols)[:, None] == jnp.arange(cols * ny)[None, :] // ny).astype(BF)
    full = jnp.dot(jnp.dot(up, block), across)
    same = jnp.arange(rows * ny)[:, None] % ny == jnp.arange(cols * ny)[None, :] % ny
    return jnp.where(same, full, jnp.zeros_like(full))


def total_of(value, axis):
    count = lax.axis_size(axis)
    stride = 1
    while stride < count:
        value = value + lax.ppermute(value, axis, [(i, i ^ stride) for i in range(count)])
        stride *= 2
    return value


def per_device(initial_state, conductivity, omega, psi, range_prev, corange_prev):
    samples, nx, ny, nz = initial_state.shape
    ranks = psi.shape[0]
    cells = samples * nx * ny * nz
    par = lax.axis_index("par")
    par_size = lax.axis_size("par")

    kfaces = faces_of(conductivity)
    ufaces = faces_of(initial_state)
    sent = [jnp.concatenate([k.astype(BF), u.astype(BF)], axis=0) for k, u in zip(kfaces, ufaces)]
    got = exchange(sent[0], sent[1], "sx") + exchange(sent[2], sent[3], "sy")
    coefs = tuple(HALF * (k + g[:samples].astype(F32)) for k, g in zip(kfaces, got))
    halos = tuple(g[samples:] for g in got)

    face_shape_x, face_shape_y = (samples, ny, nz), (samples, nx, nz)
    step_outs = [((samples, nx, ny, nz), F32)] + [(face_shape_x, F32)] * 2 + [(face_shape_y, F32)] * 2
    cost = dict(flops=24 * cells, nbytes=12 * cells)
    state = initial_state
    faces = None
    for step in range(STEPS):
        if step == 0:
            out = vmem_call(first_kernel, step_outs, "first_step", **cost)(state, conductivity)
        else:
            sent = [f.astype(BF) for f in faces]
            halos = exchange(sent[0], sent[1], "sx") + exchange(sent[2], sent[3], "sy")
            out = vmem_call(step_kernel, step_outs, "later_step", **cost)(state, conductivity, *faces)
        state = out[0]
        old = ufaces if faces is None else faces
        faces = add_fluxes(out[1:], old, coefs, halos)

    final_state, snapshot = vmem_call(
        final_kernel,
        [((samples, nx, ny, nz), F32), ((samples, nx, ny, nz), BF)],
        "final",
        scratch=[pltpu.VMEM((samples, nx, ny, nz), F32), pltpu.SemaphoreType.DMA((samples,))],
        limit=16 << 20,
        hbm_out=(0,),
        flops=cells,
        nbytes=10 * cells,
    )(state, *faces)

    other = lax.ppermute(snapshot, "par", [(i, (i + 1) % par_size) for i in range(par_size)])
    own_ranks = range_prev.shape[0]
    own_cols = lax.dynamic_slice_in_dim(omega, par * own_ranks, own_ranks, 1)
    own_rows = lax.dynamic_slice_in_dim(own_cols, par * samples, samples, 0)
    source = (par + par_size - 1) % par_size
    other_rows = lax.dynamic_slice_in_dim(own_cols, source * samples, samples, 0)
    w_own, w_other = spread(own_rows.T, ny), spread(other_rows.T, ny)

    partial_sum = vmem_call(
        corange_kernel,
        [((ranks, samples), F32)],
        "corange",
        scratch=[pltpu.VMEM((ranks * ny, samples * ny), F32)],
        limit=32 << 20,
        flops=2 * ranks * cells * ny,
        nbytes=4 * cells,
    )(psi, snapshot)[0]
    corange = corange_prev + total_of(total_of(partial_sum, "sx"), "sy")

    range_sketch = vmem_call(
        range_kernel,
        [(range_prev.shape, BF)],
        "range",
        limit=32 << 20,
        flops=4 * ranks * cells * ny,
        nbytes=8 * cells,
    )(w_own, w_other, snapshot, other, range_prev)[0]
    return final_state, range_sketch, corange


def solution(mesh):
    in_specs = (
        P("par", "sx", "sy", None),
        P("par", "sx", "sy", None),
        P(),
        P(None, "sx", "sy", None),
        P("par", "sx", "sy", None),
        P(None, "par"),
    )
    out_specs = (P("par", "sx", "sy", None), P("par", "sx", "sy", None), P(None, "par"))
    return jax.shard_map(
        per_device, mesh=mesh, in_specs=in_specs, out_specs=out_specs, check_vma=False
    )
```

```python
import functools

import jax
import jax.numpy as jnp
from jax import lax
from jax.experimental import pallas as pl
from jax.experimental.pallas import tpu as pltpu
from jax.sharding import PartitionSpec as P

STEPS = 4
BF = jnp.bfloat16
F32 = jnp.float32
HALF = 0.16 * 0.5
BLOCK = 8
ROWS = 8


def vmem_call(
    kernel, outs, name, limit=3 << 20, scratch=(), hbm_in=(), hbm_out=(), aliases=None, flops=0, nbytes=0
):
    def call(*args):
        in_specs = []
        ready = []
        for i, arg in enumerate(args):
            in_specs.append(pl.BlockSpec(memory_space=pltpu.HBM if i in hbm_in else pltpu.VMEM))
            ready.append(
                pltpu.with_memory_space_constraint(arg, pltpu.HBM if i in hbm_in else pltpu.VMEM)
            )
        out_shape = []
        out_specs = []
        for i, (shape, dtype) in enumerate(outs):
            out_shape.append((pltpu.HBM if i in hbm_out else pltpu.VMEM)(shape, dtype))
            out_specs.append(pl.BlockSpec(memory_space=pltpu.HBM if i in hbm_out else pltpu.VMEM))
        return pl.pallas_call(
            kernel,
            out_shape=out_shape,
            in_specs=in_specs,
            out_specs=out_specs,
            scratch_shapes=list(scratch),
            input_output_aliases=aliases or {},
            name=name,
            compiler_params=pltpu.CompilerParams(vmem_limit_bytes=limit),
            cost_estimate=pl.CostEstimate(flops=flops, bytes_accessed=nbytes, transcendentals=0),
        )(*ready)

    return call


def faces_kernel(u_ref, k_ref, lx, ux, ly, uy, xbuf, ybuf, sem):
    _, nx, ny, _ = u_ref.shape
    copies = []
    for i, (ref, end) in enumerate(((k_ref, 0), (u_ref, 0), (k_ref, 1), (u_ref, 1))):
        x, y = end * (nx - 1), end * (ny - 1)
        copies.append(pltpu.make_async_copy(ref.at[:, x], xbuf.at[i], sem.at[i]))
        copies.append(pltpu.make_async_copy(ref.at[:, :, y], ybuf.at[i], sem.at[4 + i]))
    for copy in copies:
        copy.start()
    for i in range(4):
        copies[2 * i].wait()
        copies[2 * i + 1].wait()
        (lx if i < 2 else ux)[i % 2] = xbuf[i].astype(BF)
        (ly if i < 2 else uy)[i % 2] = ybuf[i].astype(BF)


def y_line(ref, s, y):
    _, nx, ny, _ = ref.shape
    return pl.ds(s * (nx * ny) + y, nx, stride=ny)


def flat(ref):
    samples, nx, ny, nz = ref.shape
    return ref.reshape(samples * nx * ny, nz)


def coef_kernel(k_hbm, cx_ref, cy_ref, cup_ref, cdown_ref, kx0, kx1, ky0, ky1, buf, sem):
    samples, nx, ny, nz = k_hbm.shape
    shape = (BLOCK, ny, nz)
    groups = samples // BLOCK
    y_open = lax.broadcasted_iota(jnp.int32, shape, 1) < ny - 1
    lane = lax.broadcasted_iota(jnp.int32, shape, 2)

    def copy_of(g):
        part = pl.ds(g * BLOCK, BLOCK)
        return pltpu.make_async_copy(k_hbm.at[part], buf.at[part], sem.at[g])

    for g in range(groups):
        copy_of(g).start()
    rows = flat(buf)
    for g in range(groups):
        copy_of(g).wait()
        part = slice(g * BLOCK, (g + 1) * BLOCK)
        for s in range(g * BLOCK, (g + 1) * BLOCK):
            ky0[s] = rows[y_line(buf, s, 0), :] * HALF
            ky1[s] = rows[y_line(buf, s, ny - 1), :] * HALF
        k = buf[part, 0] * HALF
        kx0[part] = k
        for x in range(nx):
            if x + 1 < nx:
                k_next = buf[part, x + 1] * HALF
                cx_ref[part, x] = k + k_next
            cy_ref[part, x] = jnp.where(y_open, k + pltpu.roll(k, ny - 1, 1), 0.0)
            cup_ref[part, x] = k + jnp.where(lane < nz - 1, pltpu.roll(k, nz - 1, 2), 0.0)
            cdown_ref[part, x] = k + jnp.where(lane > 0, pltpu.roll(k, 1, 2), 0.0)
            if x + 1 < nx:
                k = k_next
        kx1[part] = k


def difference_matrix(nz):
    row = lax.broadcasted_iota(jnp.int32, (nz, nz), 0)
    col = lax.broadcasted_iota(jnp.int32, (nz, nz), 1)
    eye = (row == col).astype(F32)
    up = (row == col + 1).astype(F32) - eye
    down = (row + 1 == col).astype(F32) - eye
    both = jnp.concatenate([up, down], axis=1).astype(BF)
    return jnp.concatenate([both, both], axis=0)


def first_step_kernel(u_hbm, cx_ref, cy_ref, cup_ref, cdown_ref, u_ref, w_ref, sem):
    groups = u_ref.shape[0] // BLOCK

    def copy_of(g):
        part = pl.ds(g * BLOCK, BLOCK)
        return pltpu.make_async_copy(u_hbm.at[part], u_ref.at[part], sem.at[g])

    for g in range(groups):
        copy_of(g).start()
    step_body(u_ref, cx_ref, cy_ref, cup_ref, cdown_ref, w_ref, lambda g: copy_of(g).wait())


def step_kernel(u_ref, cx_ref, cy_ref, cup_ref, cdown_ref, *refs):
    step_body(u_ref, cx_ref, cy_ref, cup_ref, cdown_ref, refs[-1], lambda g: None)


def step_body(u_ref, cx_ref, cy_ref, cup_ref, cdown_ref, w_ref, before):
    samples, nx, ny, nz = u_ref.shape
    shape = (BLOCK, ny, nz)
    matrix = difference_matrix(nz)

    def body(g, carry):
        before(g)
        part = pl.ds(g * BLOCK, BLOCK)
        u = u_ref[part, 0]
        for x in range(nx):
            total = u
            if x + 1 < nx:
                u_next = u_ref[part, x + 1]
                flux = cx_ref[part, x] * (u_next - u)
                total = total + flux
            if x > 0:
                total = total - flux_low
            fy = cy_ref[part, x] * (pltpu.roll(u, ny - 1, 1) - u)
            total = total + (fy - pltpu.roll(fy, 1, 1))
            wide = u.reshape(BLOCK * ny, nz)
            coarse = wide.astype(BF)
            fine = (wide - coarse.astype(F32)).astype(BF)
            dz = jnp.dot(jnp.concatenate([coarse, fine], axis=1), matrix, preferred_element_type=F32)
            total = total + cup_ref[part, x] * dz[:, :nz].reshape(shape)
            total = total + cdown_ref[part, x] * dz[:, nz:].reshape(shape)
            w_ref[part, x] = total
            if x + 1 < nx:
                u, flux_low = u_next, flux
        return carry

    lax.fori_loop(0, samples // BLOCK, body, 0)


def edge_kernel(send, w_in, u_ref, cx0, cx1, cy0, cy1, hx0, hx1, hy0, hy1, *refs):
    del w_in
    w_ref, lx, ux, ly, uy = refs[-5:] if send else (refs[-1],) + (None,) * 4
    samples, nx, ny, nz = u_ref.shape
    w_rows, u_rows = flat(w_ref), flat(u_ref)

    def one(s):
        for y, coef, halo in ((0, cy0, hy0), (ny - 1, cy1, hy1)):
            line = y_line(u_ref, s, y)
            flux = coef[s] * (halo[s].astype(F32) - u_rows[line, :])
            w_rows[line, :] = w_rows[line, :] + flux
        for x, coef, halo, out in ((0, cx0, hx0, lx), (nx - 1, cx1, hx1, ux)):
            value = w_ref[s, x] + coef[s] * (halo[s].astype(F32) - u_ref[s, x])
            w_ref[s, x] = value
            if send:
                out[s] = value.astype(BF)
        if send:
            for y, out in ((0, ly), (ny - 1, uy)):
                out[s] = w_rows[y_line(u_ref, s, y), :].astype(BF)

    def body(i, carry):
        for j in range(4):
            one(i * 4 + j)
        return carry

    lax.fori_loop(0, samples // 4, body, 0)


def split_shape(shape):
    count, nx, ny, nz = shape
    return (nx, ny // ROWS, count * ROWS, nz)


def split_into(out_ref, x, value):
    count, ny, nz = value.shape
    for h in range(ny // ROWS):
        part = value[:, h * ROWS : (h + 1) * ROWS]
        out_ref[x, h] = part.reshape(count * ROWS, nz).astype(BF)


def one_hot(rows, cols, row_width, col_width):
    row = lax.broadcasted_iota(jnp.int32, (rows, cols), 0) // row_width
    col = lax.broadcasted_iota(jnp.int32, (rows, cols), 1) // col_width
    return (row == col).astype(BF)


def spread(block):
    rows, cols = block.shape
    tall = jnp.dot(one_hot(rows * ROWS, rows, ROWS, 1), block, preferred_element_type=F32).astype(BF)
    full = jnp.dot(tall, one_hot(cols, cols * ROWS, 1, ROWS), preferred_element_type=F32)
    row = lax.broadcasted_iota(jnp.int32, full.shape, 0) % ROWS
    col = lax.broadcasted_iota(jnp.int32, full.shape, 1) % ROWS
    return jnp.where(row == col, full, 0.0).astype(BF)


def psi_kernel(psi_hbm, omega_ref, out_ref, weight_ref, buf, sem):
    ranks, nx, ny, nz = psi_hbm.shape
    parts = 4

    def copy_of(i):
        part = pl.ds(i * (nx // parts), nx // parts)
        return pltpu.make_async_copy(psi_hbm.at[:, part], buf.at[:, part], sem.at[i])

    for i in range(parts):
        copy_of(i).start()
    for i in range(omega_ref.shape[0]):
        weight_ref[i] = spread(omega_ref[i])

    def body(x, carry):
        split_into(out_ref, x, buf[:, x].astype(F32))
        return carry

    for i in range(parts):
        copy_of(i).wait()
        lax.fori_loop(i * (nx // parts), (i + 1) * (nx // parts), body, 0)


def side_by_side(ref, x):
    return jnp.concatenate([ref[x, h] for h in range(ref.shape[1])], axis=1)


def range_kernel(weight_ref, own_ref, other_ref, prev_hbm, out_ref, done_ref, prev, buf, sem):
    ranks, nx, ny, nz = prev_hbm.shape
    parts = 4

    def prev_copy(i):
        part = pl.ds(i * (nx // parts), nx // parts)
        return pltpu.make_async_copy(prev_hbm.at[:, part], prev.at[:, part], sem.at[1, i])

    for i in range(parts):
        prev_copy(i).start()

    def copy_of(i):
        part = pl.ds(i * (nx // parts), nx // parts)
        return pltpu.make_async_copy(buf.at[:, part], out_ref.at[:, part], sem.at[0, i])

    done_ref[...] = jnp.zeros_like(done_ref)

    def body(x):
        value = jnp.dot(weight_ref[0], side_by_side(own_ref, x), preferred_element_type=F32)
        value += jnp.dot(weight_ref[1], side_by_side(other_ref, x), preferred_element_type=F32)
        halves = [
            value[:, h * nz : (h + 1) * nz].reshape(ranks, ROWS, nz) for h in range(ny // ROWS)
        ]
        total = jnp.concatenate(halves, axis=1) + prev[:, x].astype(F32)
        buf[:, x] = total.astype(BF)

    for i in range(parts):
        prev_copy(i).wait()
        for x in range(i * (nx // parts), (i + 1) * (nx // parts)):
            body(x)
        copy_of(i).start()
    for i in range(parts):
        copy_of(i).wait()


def corange_kernel(psi_ref, u_ref, snap_ref, out_ref, state_hbm, acc, sem):
    copy = pltpu.make_async_copy(u_ref, state_hbm, sem)
    copy.start()
    samples, nx, ny, nz = u_ref.shape
    ranks = psi_ref.shape[2] // ROWS
    cols = ranks * ROWS
    for x in range(0, nx, 2):
        split_into(snap_ref, x, u_ref[:, x])
        split_into(snap_ref, x + 1, u_ref[:, x + 1])
        left = jnp.concatenate([side_by_side(snap_ref, x), side_by_side(snap_ref, x + 1)], axis=1)
        right = jnp.concatenate([side_by_side(psi_ref, x), side_by_side(psi_ref, x + 1)], axis=1)
        part = lax.dot_general(left, right, (((1,), (1,)), ((), ())), preferred_element_type=F32)
        acc[...] = part if x == 0 else acc[...] + part
    row = lax.broadcasted_iota(jnp.int32, (ROWS, cols), 0)
    col = lax.broadcasted_iota(jnp.int32, (ROWS, cols), 1) % ROWS
    fold = (
        lax.broadcasted_iota(jnp.int32, (cols, ranks), 0) // ROWS
        == lax.broadcasted_iota(jnp.int32, (cols, ranks), 1)
    ).astype(F32)
    picked = jnp.where((row == col)[None], acc[...].reshape(samples, ROWS, cols), 0.0).sum(1)
    out_ref[...] = jnp.dot(picked, fold, precision=lax.Precision.HIGHEST, preferred_element_type=F32)
    copy.wait()


def swap_pairs(count, parity, par):
    partner = {}
    for i in range(parity, count - 1, 2):
        partner[i] = i + 1
        partner[i + 1] = i
    pairs = []
    for i in range(count):
        for p in range(par):
            source = i * par + p
            if i in partner:
                pairs.append((source, partner[i] * par + p))
            else:
                pairs.append((source, i * par + (p + 1) % par))
    return pairs


def exchange(low, high, axis):
    count, par = lax.axis_size(axis), lax.axis_size("par")
    index = lax.axis_index(axis)
    odd = index % 2 == 1
    first = lax.ppermute(jnp.where(odd, low, high), (axis, "par"), swap_pairs(count, 0, par))
    second = lax.ppermute(jnp.where(odd, high, low), (axis, "par"), swap_pairs(count, 1, par))
    zero = jnp.zeros_like(first)
    below = jnp.where(index == 0, zero, jnp.where(odd, first, second))
    above = jnp.where(index == count - 1, zero, jnp.where(odd, second, first))
    return below, above


def total_of(value, axis):
    count = lax.axis_size(axis)
    total = value
    for shift in range(1, count):
        total = total + lax.ppermute(value, axis, [(i, i ^ shift) for i in range(count)])
    return total


def per_device(initial_state, conductivity, omega, psi, range_prev, corange_prev):
    samples, nx, ny, nz = block = initial_state.shape
    ranks = psi.shape[0]
    cells = samples * nx * ny * nz
    x_face, y_face = (samples, ny, nz), (samples, nx, nz)
    par = lax.axis_index("par")
    par_size = lax.axis_size("par")

    sent = vmem_call(
        faces_kernel,
        [((2,) + x_face, BF)] * 2 + [((2,) + y_face, BF)] * 2,
        "faces",
        scratch=[
            pltpu.VMEM((4,) + x_face, F32),
            pltpu.VMEM((4,) + y_face, F32),
            pltpu.SemaphoreType.DMA((8,)),
        ],
        hbm_in=(0, 1),
        flops=cells // 2,
        nbytes=cells,
    )(initial_state, conductivity)
    got_y = exchange(sent[2], sent[3], "sy")
    got = exchange(sent[0], sent[1], "sx") + got_y
    halos = [g[1] for g in got]

    groups = samples // BLOCK
    made = vmem_call(
        coef_kernel,
        [(block, F32)] * 4 + [(x_face, F32)] * 2 + [(y_face, F32)] * 2,
        "coefs",
        limit=6 << 20,
        scratch=[pltpu.VMEM(block, F32), pltpu.SemaphoreType.DMA((groups,))],
        hbm_in=(0,),
        flops=12 * cells,
        nbytes=8 * cells,
    )(conductivity)
    coefs, kfaces = made[:4], made[4:]
    face_coefs = [k + HALF * g[0].astype(F32) for k, g in zip(kfaces, got)]
    own_ranks = range_prev.shape[0]
    own_cols = lax.dynamic_slice_in_dim(omega, par * own_ranks, own_ranks, 1).T
    source = (par + par_size - 1) % par_size
    omega_blocks = jnp.stack(
        [lax.dynamic_slice_in_dim(own_cols, p * samples, samples, 1) for p in (par, source)]
    )
    held_psi, weights = vmem_call(
        psi_kernel,
        [(split_shape(psi.shape), BF), ((2, own_ranks * ROWS, samples * ROWS), BF)],
        "psi",
        limit=6 << 20,
        scratch=[pltpu.VMEM(psi.shape, BF), pltpu.SemaphoreType.DMA((4,))],
        hbm_in=(0,),
        flops=4 * cells,
        nbytes=4 * cells,
    )(psi, omega_blocks)

    cost = dict(flops=24 * cells, nbytes=8 * cells)
    for step in range(STEPS):
        if step == 0:
            state, moved = vmem_call(
                first_step_kernel,
                [(block, F32)] * 2,
                "first_step",
                scratch=[pltpu.SemaphoreType.DMA((groups,))],
                hbm_in=(0,),
                **cost,
            )(initial_state, *coefs)
        else:
            got_y = exchange(edges[2], edges[3], "sy")
            halos = exchange(edges[0], edges[1], "sx") + got_y
            moved = vmem_call(step_kernel, [(block, F32)], "step", **cost)(state, *coefs, held_psi, weights)[0]
        send = step < STEPS - 1
        state, *edges = vmem_call(
            functools.partial(edge_kernel, send),
            [(block, F32)] + [(x_face, BF), (x_face, BF), (y_face, BF), (y_face, BF)] * send,
            "edge",
            aliases={0: 0},
            flops=cells,
            nbytes=cells,
        )(moved, state, *face_coefs, *halos, held_psi, weights)

    snapshot, partial_sum, final_state = vmem_call(
        corange_kernel,
        [(split_shape(block), BF), ((samples, ranks), F32), (block, F32)],
        "corange",
        limit=6 << 20,
        scratch=[pltpu.VMEM((samples * ROWS, ranks * ROWS), F32), pltpu.SemaphoreType.DMA],
        hbm_out=(2,),
        flops=2 * ranks * ROWS * cells,
        nbytes=4 * cells,
    )(held_psi, state)
    other = lax.ppermute(snapshot, "par", [(i, (i + 1) % par_size) for i in range(par_size)])
    range_sketch, done = vmem_call(
        range_kernel,
        [(range_prev.shape, BF), ((samples, ranks), F32)],
        "range",
        limit=8 << 20,
        scratch=[
            pltpu.VMEM(range_prev.shape, BF),
            pltpu.VMEM(range_prev.shape, BF),
            pltpu.SemaphoreType.DMA((2, 4)),
        ],
        hbm_in=(3,),
        hbm_out=(0,),
        flops=2 * ranks * ROWS * cells,
        nbytes=4 * cells,
    )(weights, snapshot, other, range_prev)
    corange = corange_prev.T + total_of(total_of(partial_sum, "sx") + done, "sy")
    return final_state, range_sketch, corange.T


def solution(mesh):
    in_specs = (
        P("par", "sx", "sy", None),
        P("par", "sx", "sy", None),
        P(),
        P(None, "sx", "sy", None),
        P("par", "sx", "sy", None),
        P(None, "par"),
    )
    out_specs = (P("par", "sx", "sy", None), P("par", "sx", "sy", None), P(None, "par"))
    return jax.shard_map(
        per_device, mesh=mesh, in_specs=in_specs, out_specs=out_specs, check_vma=False
    )
```

```python
import functools

import jax
import jax.numpy as jnp
from jax import lax
from jax.experimental import pallas as pl
from jax.experimental.pallas import tpu as pltpu
from jax.sharding import PartitionSpec as P

STEPS = 4
BF = jnp.bfloat16
F32 = jnp.float32
HALF = 0.16 * 0.5
BLOCK = 8
ROWS = 8


def vmem_call(
    kernel, outs, name, limit=3 << 20, scratch=(), hbm_in=(), hbm_out=(), aliases=None, flops=0, nbytes=0
):
    def call(*args):
        in_specs = []
        ready = []
        for i, arg in enumerate(args):
            in_specs.append(pl.BlockSpec(memory_space=pltpu.HBM if i in hbm_in else pltpu.VMEM))
            ready.append(
                pltpu.with_memory_space_constraint(arg, pltpu.HBM if i in hbm_in else pltpu.VMEM)
            )
        out_shape = []
        out_specs = []
        for i, (shape, dtype) in enumerate(outs):
            out_shape.append((pltpu.HBM if i in hbm_out else pltpu.VMEM)(shape, dtype))
            out_specs.append(pl.BlockSpec(memory_space=pltpu.HBM if i in hbm_out else pltpu.VMEM))
        return pl.pallas_call(
            kernel,
            out_shape=out_shape,
            in_specs=in_specs,
            out_specs=out_specs,
            scratch_shapes=list(scratch),
            input_output_aliases=aliases or {},
            name=name,
            compiler_params=pltpu.CompilerParams(vmem_limit_bytes=limit),
            cost_estimate=pl.CostEstimate(flops=flops, bytes_accessed=nbytes, transcendentals=0),
        )(*ready)

    return call


def faces_kernel(u_ref, k_ref, lx, ux, ly, uy, xbuf, ybuf, sem):
    _, nx, ny, _ = u_ref.shape
    copies = []
    for i, (ref, end) in enumerate(((k_ref, 0), (u_ref, 0), (k_ref, 1), (u_ref, 1))):
        x, y = end * (nx - 1), end * (ny - 1)
        copies.append(pltpu.make_async_copy(ref.at[:, x], xbuf.at[i], sem.at[i]))
        copies.append(pltpu.make_async_copy(ref.at[:, :, y], ybuf.at[i], sem.at[4 + i]))
    for copy in copies:
        copy.start()
    for i in range(4):
        copies[2 * i].wait()
        copies[2 * i + 1].wait()
        (lx if i < 2 else ux)[i % 2] = xbuf[i].astype(BF)
        (ly if i < 2 else uy)[i % 2] = ybuf[i].astype(BF)


def y_line(ref, s, y):
    _, nx, ny, _ = ref.shape
    return pl.ds(s * (nx * ny) + y, nx, stride=ny)


def flat(ref):
    samples, nx, ny, nz = ref.shape
    return ref.reshape(samples * nx * ny, nz)


def first_kernel(
    u_hbm, k_hbm, u_ref, w_ref, cx_ref, cy_ref, cup_ref, cdown_ref, kx0, kx1, ky0, ky1, buf, sem
):
    samples, nx, ny, nz = u_ref.shape
    shape = (BLOCK, ny, nz)
    groups = samples // BLOCK
    y_open = lax.broadcasted_iota(jnp.int32, shape, 1) < ny - 1
    lane = lax.broadcasted_iota(jnp.int32, shape, 2)
    rows = flat(buf)

    def copies(g):
        part = pl.ds(g * BLOCK, BLOCK)
        return (
            pltpu.make_async_copy(k_hbm.at[part], buf.at[part], sem.at[0, g]),
            pltpu.make_async_copy(u_hbm.at[part], u_ref.at[part], sem.at[1, g]),
        )

    for g in range(groups):
        for copy in copies(g):
            copy.start()

    def before(g):
        for copy in copies(g):
            copy.wait()
        part = pl.ds(g * BLOCK, BLOCK)
        for i in range(BLOCK):
            s = g * BLOCK + i
            ky0[s] = rows[y_line(buf, s, 0), :] * HALF
            ky1[s] = rows[y_line(buf, s, ny - 1), :] * HALF
        k = buf[part, 0] * HALF
        kx0[part] = k
        for x in range(nx):
            if x + 1 < nx:
                k_next = buf[part, x + 1] * HALF
                cx_ref[part, x] = k + k_next
            cy_ref[part, x] = jnp.where(y_open, k + pltpu.roll(k, ny - 1, 1), 0.0)
            cup_ref[part, x] = k + jnp.where(lane < nz - 1, pltpu.roll(k, nz - 1, 2), 0.0)
            cdown_ref[part, x] = k + jnp.where(lane > 0, pltpu.roll(k, 1, 2), 0.0)
            if x + 1 < nx:
                k = k_next
        kx1[part] = k

    step_body(u_ref, cx_ref, cy_ref, cup_ref, cdown_ref, w_ref, before)


def difference_matrix(nz):
    row = lax.broadcasted_iota(jnp.int32, (nz, nz), 0)
    col = lax.broadcasted_iota(jnp.int32, (nz, nz), 1)
    eye = (row == col).astype(F32)
    up = (row == col + 1).astype(F32) - eye
    down = (row + 1 == col).astype(F32) - eye
    both = jnp.concatenate([up, down], axis=1).astype(BF)
    return jnp.concatenate([both, both], axis=0)


def step_kernel(u_ref, cx_ref, cy_ref, cup_ref, cdown_ref, *refs):
    step_body(u_ref, cx_ref, cy_ref, cup_ref, cdown_ref, refs[-1])


def last_step_kernel(u_ref, cx_ref, cy_ref, cup_ref, cdown_ref, *refs):
    w_ref, state_hbm, sem = refs[-3:]
    half = u_ref.shape[0] // BLOCK // 2

    def copy_of(g):
        part = pl.ds(g * BLOCK, BLOCK)
        return pltpu.make_async_copy(w_ref.at[part], state_hbm.at[part], sem.at[g])

    def after(g):
        @pl.when(g < half)
        def _():
            copy_of(g).start()

    step_body(u_ref, cx_ref, cy_ref, cup_ref, cdown_ref, w_ref, after=after)
    for g in range(half):
        copy_of(g).wait()


def step_body(u_ref, cx_ref, cy_ref, cup_ref, cdown_ref, w_ref, before=None, after=None):
    samples, nx, ny, nz = u_ref.shape
    shape = (BLOCK, ny, nz)
    matrix = difference_matrix(nz)

    def body(g, carry):
        if before:
            before(g)
        part = pl.ds(g * BLOCK, BLOCK)
        u = u_ref[part, 0]
        for x in range(nx):
            total = u
            if x + 1 < nx:
                u_next = u_ref[part, x + 1]
                flux = cx_ref[part, x] * (u_next - u)
                total = total + flux
            if x > 0:
                total = total - flux_low
            fy = cy_ref[part, x] * (pltpu.roll(u, ny - 1, 1) - u)
            total = total + (fy - pltpu.roll(fy, 1, 1))
            wide = u.reshape(BLOCK * ny, nz)
            coarse = wide.astype(BF)
            fine = (wide - coarse.astype(F32)).astype(BF)
            dz = jnp.dot(jnp.concatenate([coarse, fine], axis=1), matrix, preferred_element_type=F32)
            total = total + cup_ref[part, x] * dz[:, :nz].reshape(shape)
            total = total + cdown_ref[part, x] * dz[:, nz:].reshape(shape)
            w_ref[part, x] = total
            if x + 1 < nx:
                u, flux_low = u_next, flux
        if after:
            after(g)
        return carry

    lax.fori_loop(0, samples // BLOCK, body, 0)


def edge_kernel(send, w_in, u_ref, cx0, cx1, cy0, cy1, hx0, hx1, hy0, hy1, *refs):
    del w_in
    w_ref, lx, ux, ly, uy = refs[-5:] if send else (refs[-1],) + (None,) * 4
    samples, nx, ny, nz = u_ref.shape
    w_rows, u_rows = flat(w_ref), flat(u_ref)

    def one(s):
        for y, coef, halo in ((0, cy0, hy0), (ny - 1, cy1, hy1)):
            line = y_line(u_ref, s, y)
            flux = coef[s] * (halo[s].astype(F32) - u_rows[line, :])
            w_rows[line, :] = w_rows[line, :] + flux
        for x, coef, halo, out in ((0, cx0, hx0, lx), (nx - 1, cx1, hx1, ux)):
            value = w_ref[s, x] + coef[s] * (halo[s].astype(F32) - u_ref[s, x])
            w_ref[s, x] = value
            if send:
                out[s] = value.astype(BF)
        if send:
            for y, out in ((0, ly), (ny - 1, uy)):
                out[s] = w_rows[y_line(u_ref, s, y), :].astype(BF)

    def body(i, carry):
        for j in range(4):
            one(i * 4 + j)
        return carry

    lax.fori_loop(0, samples // 4, body, 0)


def split_shape(shape):
    count, nx, ny, nz = shape
    return (nx, ny // ROWS, count * ROWS, nz)


def split_into(out_ref, x, value):
    count, ny, nz = value.shape
    for h in range(ny // ROWS):
        part = value[:, h * ROWS : (h + 1) * ROWS]
        out_ref[x, h] = part.reshape(count * ROWS, nz).astype(BF)


def one_hot(rows, cols, row_width, col_width):
    row = lax.broadcasted_iota(jnp.int32, (rows, cols), 0) // row_width
    col = lax.broadcasted_iota(jnp.int32, (rows, cols), 1) // col_width
    return (row == col).astype(BF)


def spread(block):
    rows, cols = block.shape
    tall = jnp.dot(one_hot(rows * ROWS, rows, ROWS, 1), block, preferred_element_type=F32).astype(BF)
    full = jnp.dot(tall, one_hot(cols, cols * ROWS, 1, ROWS), preferred_element_type=F32)
    row = lax.broadcasted_iota(jnp.int32, full.shape, 0) % ROWS
    col = lax.broadcasted_iota(jnp.int32, full.shape, 1) % ROWS
    return jnp.where(row == col, full, 0.0).astype(BF)


def psi_kernel(psi_hbm, prev_hbm, omega_ref, out_ref, x_ref, y_ref, weight_ref, prev_ref, buf, wide, sem):
    ranks, nx, ny, nz = psi_hbm.shape
    parts = 4
    rows = wide.reshape(ranks * ny, nz)

    def line(y):
        return rows[pl.ds(y, ranks, stride=ny), :].astype(BF)

    def copy_of(i):
        part = pl.ds(i * (nx // parts), nx // parts)
        return pltpu.make_async_copy(psi_hbm.at[:, part], buf.at[:, part], sem.at[i])

    for i in range(parts):
        copy_of(i).start()
    prev_copy = pltpu.make_async_copy(prev_hbm, prev_ref, sem.at[parts])
    prev_copy.start()
    for i in range(omega_ref.shape[0]):
        weight_ref[i] = spread(omega_ref[i])

    def body(x, carry):
        value = buf[:, x].astype(F32)
        split_into(out_ref, x, value)
        wide[...] = value
        y_ref[0, x] = line(0)
        y_ref[1, x] = line(ny - 1)
        return carry

    for i in range(parts):
        copy_of(i).wait()
        lax.fori_loop(i * (nx // parts), (i + 1) * (nx // parts), body, 0)
    for end in range(2):
        wide[...] = buf[:, end * (nx - 1)].astype(F32)
        for y in range(ny):
            x_ref[end, y] = line(y)
    prev_copy.wait()


def side_by_side(ref, x):
    return jnp.concatenate([ref[x, h] for h in range(ref.shape[1])], axis=1)


def range_kernel(
    weight_ref, own_ref, other_ref, prev_ref, u_ref, state_in, out_ref, state_hbm, done_ref, buf, sem
):
    del state_in
    ranks, nx, ny, nz = prev_ref.shape
    parts = 4
    inner = pl.ds(1, nx - 2)
    copies = []
    for i, (x, y) in enumerate(((0, 0), (nx - 1, ny - 1))):
        copies.append(pltpu.make_async_copy(u_ref.at[:, x], state_hbm.at[:, x], sem.at[1, i]))
        copies.append(
            pltpu.make_async_copy(u_ref.at[:, inner, y], state_hbm.at[:, inner, y], sem.at[1, 2 + i])
        )
    for copy in copies:
        copy.start()
    done_ref[...] = jnp.zeros_like(done_ref)

    def copy_of(i):
        part = pl.ds(i * (nx // parts), nx // parts)
        return pltpu.make_async_copy(buf.at[:, part], out_ref.at[:, part], sem.at[0, i])

    for i in range(parts):
        for x in range(i * (nx // parts), (i + 1) * (nx // parts)):
            value = jnp.dot(weight_ref[0], side_by_side(own_ref, x), preferred_element_type=F32)
            value += jnp.dot(weight_ref[1], side_by_side(other_ref, x), preferred_element_type=F32)
            halves = [
                value[:, h * nz : (h + 1) * nz].reshape(ranks, ROWS, nz) for h in range(ny // ROWS)
            ]
            total = jnp.concatenate(halves, axis=1) + prev_ref[:, x].astype(F32)
            buf[:, x] = total.astype(BF)
        copy_of(i).start()
    for i in range(parts):
        copy_of(i).wait()
    for copy in copies:
        copy.wait()


def corange_kernel(psi_ref, u_ref, state_in, out_ref, state_hbm, snap, acc, sem):
    del state_in
    samples, nx, ny, nz = u_ref.shape
    part = pl.ds(samples // 2, samples // 2)
    copy = pltpu.make_async_copy(u_ref.at[part], state_hbm.at[part], sem)
    copy.start()
    ranks = psi_ref.shape[2] // ROWS
    cols = ranks * ROWS
    for x in range(0, nx, 2):
        split_into(snap, x, u_ref[:, x])
        split_into(snap, x + 1, u_ref[:, x + 1])
        left = jnp.concatenate([side_by_side(snap, x), side_by_side(snap, x + 1)], axis=1)
        right = jnp.concatenate([side_by_side(psi_ref, x), side_by_side(psi_ref, x + 1)], axis=1)
        part = contract(left, right)
        acc[...] = part if x == 0 else acc[...] + part
    row = lax.broadcasted_iota(jnp.int32, (ROWS, cols), 0)
    col = lax.broadcasted_iota(jnp.int32, (ROWS, cols), 1) % ROWS
    fold = (
        lax.broadcasted_iota(jnp.int32, (cols, ranks), 0) // ROWS
        == lax.broadcasted_iota(jnp.int32, (cols, ranks), 1)
    ).astype(F32)
    picked = jnp.where((row == col)[None], acc[...].reshape(samples, ROWS, cols), 0.0).sum(1)
    out_ref[...] = jnp.dot(picked, fold, precision=lax.Precision.HIGHEST, preferred_element_type=F32)
    copy.wait()


def contract(left, right):
    return lax.dot_general(left, right, (((1,), (1,)), ((), ())), preferred_element_type=F32)


def corange_faces_kernel(
    main_ref, px, py, u_ref, cx0, cx1, cy0, cy1, hx0, hx1, hy0, hy1, out_ref, xbuf, ybuf
):
    samples, nx, ny, nz = u_ref.shape
    rows = flat(u_ref)
    for end, x, coef, halo in ((0, 0, cx0, hx0), (1, nx - 1, cx1, hx1)):
        xbuf[end] = coef[...] * (halo[...].astype(F32) - u_ref[:, x])
    for end, y, coef, halo in ((0, 0, cy0, hy0), (1, ny - 1, cy1, hy1)):
        for s in range(samples):
            ybuf[end, s] = coef[s] * (halo[s].astype(F32) - rows[y_line(u_ref, s, y), :])
    total = main_ref[...]
    for buf, psi in ((xbuf, px), (ybuf, py)):
        count = buf.shape[2]
        lines = buf.reshape(2 * samples * count, nz)
        for i in range(count):
            left = [
                lines[pl.ds(end * samples * count + i, samples, stride=count), :].astype(BF)
                for end in range(2)
            ]
            right = [psi[end, i] for end in range(2)]
            total = total + contract(jnp.concatenate(left, axis=1), jnp.concatenate(right, axis=1))
    out_ref[...] = total


def finish_kernel(*refs):
    w_ref, snap_ref = refs[-2:]
    edge_kernel(False, *refs[:-1])
    nx = w_ref.shape[1]

    def body(x, carry):
        split_into(snap_ref, x, w_ref[:, x])
        return carry

    lax.fori_loop(0, nx, body, 0)


def swap_pairs(count, parity, par):
    partner = {}
    for i in range(parity, count - 1, 2):
        partner[i] = i + 1
        partner[i + 1] = i
    pairs = []
    for i in range(count):
        for p in range(par):
            source = i * par + p
            if i in partner:
                pairs.append((source, partner[i] * par + p))
            else:
                pairs.append((source, i * par + (p + 1) % par))
    return pairs


ORDER = (("sy", 0), ("sy", 1), ("sx", 0), ("sx", 1))


def exchange(faces):
    ends = {"sx": faces[:2], "sy": faces[2:]}
    par = lax.axis_size("par")
    got = {}
    for axis, parity in ORDER:
        low, high = ends[axis]
        odd = lax.axis_index(axis) % 2 == 1
        mine = jnp.where(odd, high, low) if parity else jnp.where(odd, low, high)
        pairs = swap_pairs(lax.axis_size(axis), parity, par)
        got[axis, parity] = lax.ppermute(mine, (axis, "par"), pairs)
    halos = []
    for axis in ("sx", "sy"):
        index, count = lax.axis_index(axis), lax.axis_size(axis)
        odd = index % 2 == 1
        first, second = got[axis, 0], got[axis, 1]
        zero = jnp.zeros_like(first)
        halos.append(jnp.where(index == 0, zero, jnp.where(odd, first, second)))
        halos.append(jnp.where(index == count - 1, zero, jnp.where(odd, second, first)))
    return halos


def received(value, axis):
    count = lax.axis_size(axis)
    return [lax.ppermute(value, axis, [(i, i ^ shift) for i in range(count)]) for shift in range(1, count)]


def per_device(initial_state, conductivity, omega, psi, range_prev, corange_prev):
    samples, nx, ny, nz = block = initial_state.shape
    ranks = psi.shape[0]
    cells = samples * nx * ny * nz
    x_face, y_face = (samples, ny, nz), (samples, nx, nz)
    par = lax.axis_index("par")
    par_size = lax.axis_size("par")

    sent = vmem_call(
        faces_kernel,
        [((2,) + x_face, BF)] * 2 + [((2,) + y_face, BF)] * 2,
        "faces",
        scratch=[
            pltpu.VMEM((4,) + x_face, F32),
            pltpu.VMEM((4,) + y_face, F32),
            pltpu.SemaphoreType.DMA((8,)),
        ],
        hbm_in=(0, 1),
        flops=cells // 2,
        nbytes=cells,
    )(initial_state, conductivity)
    got = exchange(sent)
    halos = [g[1] for g in got]

    groups = samples // BLOCK
    state, moved, *made = vmem_call(
        first_kernel,
        [(block, F32)] * 6 + [(x_face, F32)] * 2 + [(y_face, F32)] * 2,
        "first",
        limit=7 << 20,
        scratch=[pltpu.VMEM(block, F32), pltpu.SemaphoreType.DMA((2, groups))],
        hbm_in=(0, 1),
        flops=36 * cells,
        nbytes=16 * cells,
    )(initial_state, conductivity)
    coefs, kfaces = made[:4], made[4:]
    face_coefs = [k + HALF * g[0].astype(F32) for k, g in zip(kfaces, got)]

    own_ranks = range_prev.shape[0]
    own_cols = lax.dynamic_slice_in_dim(omega, par * own_ranks, own_ranks, 1).T
    source = (par + par_size - 1) % par_size
    omega_blocks = jnp.stack(
        [lax.dynamic_slice_in_dim(own_cols, p * samples, samples, 1) for p in (par, source)]
    )
    held_psi, psi_x, psi_y, weights, prev = vmem_call(
        psi_kernel,
        [
            (split_shape(psi.shape), BF),
            ((2, ny, ranks, nz), BF),
            ((2, nx, ranks, nz), BF),
            ((2, own_ranks * ROWS, samples * ROWS), BF),
            (range_prev.shape, BF),
        ],
        "psi",
        limit=7 << 20,
        scratch=[
            pltpu.VMEM(psi.shape, BF),
            pltpu.VMEM((ranks, ny, nz), F32),
            pltpu.SemaphoreType.DMA((5,)),
        ],
        hbm_in=(0, 1),
        flops=4 * cells,
        nbytes=4 * cells,
    )(psi, range_prev, omega_blocks)
    kept = (held_psi, psi_x, psi_y, weights, prev)

    for step in range(STEPS):
        if step > 0:
            halos = exchange(edges)
            last = step == STEPS - 1
            moved, *written = vmem_call(
                last_step_kernel if last else step_kernel,
                [(block, F32)] * (2 if last else 1),
                "step",
                scratch=[pltpu.SemaphoreType.DMA((groups,))] if last else [],
                hbm_out=(1,),
                flops=24 * cells,
                nbytes=8 * cells,
            )(state, *coefs, *kept)
        if step < STEPS - 1:
            state, *edges = vmem_call(
                functools.partial(edge_kernel, True),
                [(block, F32), (x_face, BF), (x_face, BF), (y_face, BF), (y_face, BF)],
                "edge",
                aliases={0: 0},
                flops=cells,
                nbytes=cells,
            )(moved, state, *face_coefs, *halos, *kept)

    main, written = vmem_call(
        corange_kernel,
        [((samples, ranks), F32), (block, F32)],
        "corange",
        limit=6 << 20,
        scratch=[
            pltpu.VMEM(split_shape(block), BF),
            pltpu.VMEM((samples * ROWS, ranks * ROWS), F32),
            pltpu.SemaphoreType.DMA,
        ],
        hbm_in=(2,),
        hbm_out=(1,),
        aliases={2: 1},
        flops=2 * ranks * ROWS * cells,
        nbytes=4 * cells,
    )(held_psi, moved, *written)
    partial_sum = vmem_call(
        corange_faces_kernel,
        [((samples, ranks), F32)],
        "corange_faces",
        scratch=[pltpu.VMEM((2,) + x_face, F32), pltpu.VMEM((2,) + y_face, F32)],
        flops=cells,
        nbytes=cells,
    )(main, psi_x, psi_y, state, *face_coefs, *halos)[0]
    first_sums = received(partial_sum, "sx")
    final, snapshot = vmem_call(
        finish_kernel,
        [(block, F32), (split_shape(block), BF)],
        "finish",
        aliases={0: 0},
        flops=cells,
        nbytes=2 * cells,
    )(moved, state, *face_coefs, *halos, prev, weights, partial_sum)
    other = lax.ppermute(snapshot, "par", [(i, (i + 1) % par_size) for i in range(par_size)])
    range_sketch, final_state, done = vmem_call(
        range_kernel,
        [(range_prev.shape, BF), (block, F32), ((samples, ranks), F32)],
        "range",
        limit=6 << 20,
        scratch=[pltpu.VMEM(range_prev.shape, BF), pltpu.SemaphoreType.DMA((2, 4))],
        hbm_in=(5,),
        hbm_out=(0, 1),
        aliases={5: 1},
        flops=2 * ranks * ROWS * cells,
        nbytes=4 * cells,
    )(weights, snapshot, other, prev, final, written)
    line_sum = sum(first_sums, partial_sum) + done
    corange = sum(received(line_sum, "sy"), corange_prev.T + line_sum)
    return final_state, range_sketch, corange.T


def solution(mesh):
    in_specs = (
        P("par", "sx", "sy", None),
        P("par", "sx", "sy", None),
        P(),
        P(None, "sx", "sy", None),
        P("par", "sx", "sy", None),
        P(None, "par"),
    )
    out_specs = (P("par", "sx", "sy", None), P("par", "sx", "sy", None), P(None, "par"))
    return jax.shard_map(
        per_device, mesh=mesh, in_specs=in_specs, out_specs=out_specs, check_vma=False
    )
```

```python
import functools

import jax
import jax.numpy as jnp
from jax import lax
from jax.experimental import pallas as pl
from jax.experimental.pallas import tpu as pltpu
from jax.sharding import PartitionSpec as P

STEPS = 4
BF = jnp.bfloat16
F32 = jnp.float32
HALF = 0.16 * 0.5
BLOCK = 8
ROWS = 8
SUM_COST = 20 << 20


def vmem_call(
    kernel, outs, name, limit=3 << 20, scratch=(), hbm_in=(), hbm_out=(), aliases=None, flops=0, nbytes=0
):
    def call(*args):
        in_specs = []
        ready = []
        for i, arg in enumerate(args):
            in_specs.append(pl.BlockSpec(memory_space=pltpu.HBM if i in hbm_in else pltpu.VMEM))
            ready.append(
                pltpu.with_memory_space_constraint(arg, pltpu.HBM if i in hbm_in else pltpu.VMEM)
            )
        out_shape = []
        out_specs = []
        for i, (shape, dtype) in enumerate(outs):
            out_shape.append((pltpu.HBM if i in hbm_out else pltpu.VMEM)(shape, dtype))
            out_specs.append(pl.BlockSpec(memory_space=pltpu.HBM if i in hbm_out else pltpu.VMEM))
        return pl.pallas_call(
            kernel,
            out_shape=out_shape,
            in_specs=in_specs,
            out_specs=out_specs,
            scratch_shapes=list(scratch),
            input_output_aliases=aliases or {},
            name=name,
            compiler_params=pltpu.CompilerParams(vmem_limit_bytes=limit),
            cost_estimate=pl.CostEstimate(flops=flops, bytes_accessed=nbytes, transcendentals=0),
        )(*ready)

    return call


def faces_kernel(u_ref, k_ref, lx, ux, ly, uy, xbuf, ybuf, sem):
    _, nx, ny, _ = u_ref.shape
    copies = []
    for i, (ref, end) in enumerate(((k_ref, 0), (u_ref, 0), (k_ref, 1), (u_ref, 1))):
        x, y = end * (nx - 1), end * (ny - 1)
        copies.append(pltpu.make_async_copy(ref.at[:, x], xbuf.at[i], sem.at[i]))
        copies.append(pltpu.make_async_copy(ref.at[:, :, y], ybuf.at[i], sem.at[4 + i]))
    for copy in copies:
        copy.start()
    for i in range(4):
        copies[2 * i].wait()
        copies[2 * i + 1].wait()
        (lx if i < 2 else ux)[i % 2] = xbuf[i].astype(BF)
        (ly if i < 2 else uy)[i % 2] = ybuf[i].astype(BF)


def y_line(ref, s, y):
    _, nx, ny, _ = ref.shape
    return pl.ds(s * (nx * ny) + y, nx, stride=ny)


def flat(ref):
    samples, nx, ny, nz = ref.shape
    return ref.reshape(samples * nx * ny, nz)


def first_kernel(
    u_hbm, k_hbm, u_ref, w_ref, cx_ref, cy_ref, cup_ref, cdown_ref, kx0, kx1, ky0, ky1, buf, sem
):
    samples, nx, ny, nz = u_ref.shape
    shape = (BLOCK, ny, nz)
    groups = samples // BLOCK
    y_open = lax.broadcasted_iota(jnp.int32, shape, 1) < ny - 1
    lane = lax.broadcasted_iota(jnp.int32, shape, 2)
    rows = flat(buf)

    def copies(g):
        part = pl.ds(g * BLOCK, BLOCK)
        return (
            pltpu.make_async_copy(k_hbm.at[part], buf.at[part], sem.at[0, g]),
            pltpu.make_async_copy(u_hbm.at[part], u_ref.at[part], sem.at[1, g]),
        )

    for g in range(groups):
        for copy in copies(g):
            copy.start()

    def before(g):
        for copy in copies(g):
            copy.wait()
        part = pl.ds(g * BLOCK, BLOCK)
        for i in range(BLOCK):
            s = g * BLOCK + i
            ky0[s] = rows[y_line(buf, s, 0), :] * HALF
            ky1[s] = rows[y_line(buf, s, ny - 1), :] * HALF
        k = buf[part, 0] * HALF
        kx0[part] = k
        for x in range(nx):
            if x + 1 < nx:
                k_next = buf[part, x + 1] * HALF
                cx_ref[part, x] = k + k_next
            cy_ref[part, x] = jnp.where(y_open, k + pltpu.roll(k, ny - 1, 1), 0.0)
            cup_ref[part, x] = k + jnp.where(lane < nz - 1, pltpu.roll(k, nz - 1, 2), 0.0)
            cdown_ref[part, x] = k + jnp.where(lane > 0, pltpu.roll(k, 1, 2), 0.0)
            if x + 1 < nx:
                k = k_next
        kx1[part] = k

    step_body(u_ref, cx_ref, cy_ref, cup_ref, cdown_ref, w_ref, before)


def difference_matrix(nz):
    row = lax.broadcasted_iota(jnp.int32, (nz, nz), 0)
    col = lax.broadcasted_iota(jnp.int32, (nz, nz), 1)
    eye = (row == col).astype(F32)
    up = (row == col + 1).astype(F32) - eye
    down = (row + 1 == col).astype(F32) - eye
    both = jnp.concatenate([up, down], axis=1).astype(BF)
    return jnp.concatenate([both, both], axis=0)


def step_kernel(u_ref, cx_ref, cy_ref, cup_ref, cdown_ref, *refs):
    step_body(u_ref, cx_ref, cy_ref, cup_ref, cdown_ref, refs[-1])


def last_step_kernel(u_ref, cx_ref, cy_ref, cup_ref, cdown_ref, *refs):
    w_ref, state_hbm, sem = refs[-3:]
    half = u_ref.shape[0] // BLOCK // 2

    def copy_of(g):
        part = pl.ds(g * BLOCK, BLOCK)
        return pltpu.make_async_copy(w_ref.at[part], state_hbm.at[part], sem.at[g])

    def after(g):
        @pl.when(g < half)
        def _():
            copy_of(g).start()

    step_body(u_ref, cx_ref, cy_ref, cup_ref, cdown_ref, w_ref, after=after)
    for g in range(half):
        copy_of(g).wait()


def step_body(u_ref, cx_ref, cy_ref, cup_ref, cdown_ref, w_ref, before=None, after=None):
    samples, nx, ny, nz = u_ref.shape
    shape = (BLOCK, ny, nz)
    matrix = difference_matrix(nz)

    def body(g, carry):
        if before:
            before(g)
        part = pl.ds(g * BLOCK, BLOCK)
        u = u_ref[part, 0]
        for x in range(nx):
            total = u
            if x + 1 < nx:
                u_next = u_ref[part, x + 1]
                flux = cx_ref[part, x] * (u_next - u)
                total = total + flux
            if x > 0:
                total = total - flux_low
            fy = cy_ref[part, x] * (pltpu.roll(u, ny - 1, 1) - u)
            total = total + (fy - pltpu.roll(fy, 1, 1))
            wide = u.reshape(BLOCK * ny, nz)
            coarse = wide.astype(BF)
            fine = (wide - coarse.astype(F32)).astype(BF)
            dz = jnp.dot(jnp.concatenate([coarse, fine], axis=1), matrix, preferred_element_type=F32)
            total = total + cup_ref[part, x] * dz[:, :nz].reshape(shape)
            total = total + cdown_ref[part, x] * dz[:, nz:].reshape(shape)
            w_ref[part, x] = total
            if x + 1 < nx:
                u, flux_low = u_next, flux
        if after:
            after(g)
        return carry

    lax.fori_loop(0, samples // BLOCK, body, 0)


def edge_kernel(send, w_in, u_ref, cx0, cx1, cy0, cy1, hx0, hx1, hy0, hy1, *refs):
    del w_in
    w_ref, lx, ux, ly, uy = refs[-5:] if send else (refs[-1],) + (None,) * 4
    samples, nx, ny, nz = u_ref.shape
    w_rows, u_rows = flat(w_ref), flat(u_ref)

    def one(s):
        for y, coef, halo in ((0, cy0, hy0), (ny - 1, cy1, hy1)):
            line = y_line(u_ref, s, y)
            flux = coef[s] * (halo[s].astype(F32) - u_rows[line, :])
            w_rows[line, :] = w_rows[line, :] + flux
        for x, coef, halo, out in ((0, cx0, hx0, lx), (nx - 1, cx1, hx1, ux)):
            value = w_ref[s, x] + coef[s] * (halo[s].astype(F32) - u_ref[s, x])
            w_ref[s, x] = value
            if send:
                out[s] = value.astype(BF)
        if send:
            for y, out in ((0, ly), (ny - 1, uy)):
                out[s] = w_rows[y_line(u_ref, s, y), :].astype(BF)

    def body(i, carry):
        for j in range(4):
            one(i * 4 + j)
        return carry

    lax.fori_loop(0, samples // 4, body, 0)


def split_shape(shape):
    count, nx, ny, nz = shape
    return (nx, ny // ROWS, count * ROWS, nz)


def split_into(out_ref, x, value):
    count, ny, nz = value.shape
    for h in range(ny // ROWS):
        part = value[:, h * ROWS : (h + 1) * ROWS]
        out_ref[x, h] = part.reshape(count * ROWS, nz).astype(BF)


def one_hot(rows, cols, row_width, col_width):
    row = lax.broadcasted_iota(jnp.int32, (rows, cols), 0) // row_width
    col = lax.broadcasted_iota(jnp.int32, (rows, cols), 1) // col_width
    return (row == col).astype(BF)


def spread(block):
    rows, cols = block.shape
    tall = jnp.dot(one_hot(rows * ROWS, rows, ROWS, 1), block, preferred_element_type=F32).astype(BF)
    full = jnp.dot(tall, one_hot(cols, cols * ROWS, 1, ROWS), preferred_element_type=F32)
    row = lax.broadcasted_iota(jnp.int32, full.shape, 0) % ROWS
    col = lax.broadcasted_iota(jnp.int32, full.shape, 1) % ROWS
    return jnp.where(row == col, full, 0.0).astype(BF)


def lines_kernel(psi_hbm, prev_hbm, omega_ref, after, x_ref, weight_ref, prev_ref, xbuf, wide, sem):
    del after
    ranks, nx, ny, nz = psi_hbm.shape
    rows = wide.reshape(ranks * ny, nz)
    copies = []
    for end in range(2):
        copies.append(
            pltpu.make_async_copy(psi_hbm.at[:, end * (nx - 1)], xbuf.at[end], sem.at[end])
        )
    copies.append(pltpu.make_async_copy(prev_hbm, prev_ref, sem.at[2]))
    for copy in copies:
        copy.start()
    for i in range(omega_ref.shape[0]):
        weight_ref[i] = spread(omega_ref[i])
    for end in range(2):
        copies[end].wait()
        wide[...] = xbuf[end].astype(F32)
        for y in range(ny):
            x_ref[end, y] = rows[pl.ds(y, ranks, stride=ny), :].astype(BF)
    copies[2].wait()


def psi_kernel(psi_hbm, out_ref, y_ref, buf, wide, sem):
    ranks, nx, ny, nz = psi_hbm.shape
    parts = 4
    rows = wide.reshape(ranks * ny, nz)

    def copy_of(i):
        part = pl.ds(i * (nx // parts), nx // parts)
        return pltpu.make_async_copy(psi_hbm.at[:, part], buf.at[:, part], sem.at[i])

    for i in range(parts):
        copy_of(i).start()

    def body(x, carry):
        value = buf[:, x].astype(F32)
        split_into(out_ref, x, value)
        wide[...] = value
        for end in range(2):
            y_ref[end, x] = rows[pl.ds(end * (ny - 1), ranks, stride=ny), :].astype(BF)
        return carry

    for i in range(parts):
        copy_of(i).wait()
        lax.fori_loop(i * (nx // parts), (i + 1) * (nx // parts), body, 0)


def side_by_side(ref, x):
    return jnp.concatenate([ref[x, h] for h in range(ref.shape[1])], axis=1)


def range_kernel(
    weight_ref, own_ref, other_ref, prev_ref, u_ref, state_in, out_ref, state_hbm, done_ref, buf, sem
):
    del state_in
    ranks, nx, ny, nz = prev_ref.shape
    parts = 4
    inner = pl.ds(1, nx - 2)
    copies = []
    for i, (x, y) in enumerate(((0, 0), (nx - 1, ny - 1))):
        copies.append(pltpu.make_async_copy(u_ref.at[:, x], state_hbm.at[:, x], sem.at[1, i]))
        copies.append(
            pltpu.make_async_copy(u_ref.at[:, inner, y], state_hbm.at[:, inner, y], sem.at[1, 2 + i])
        )
    for copy in copies:
        copy.start()
    done_ref[...] = jnp.zeros_like(done_ref)

    def copy_of(i):
        part = pl.ds(i * (nx // parts), nx // parts)
        return pltpu.make_async_copy(buf.at[:, part], out_ref.at[:, part], sem.at[0, i])

    for i in range(parts):
        for x in range(i * (nx // parts), (i + 1) * (nx // parts)):
            value = jnp.dot(weight_ref[0], side_by_side(own_ref, x), preferred_element_type=F32)
            value += jnp.dot(weight_ref[1], side_by_side(other_ref, x), preferred_element_type=F32)
            halves = [
                value[:, h * nz : (h + 1) * nz].reshape(ranks, ROWS, nz) for h in range(ny // ROWS)
            ]
            total = jnp.concatenate(halves, axis=1) + prev_ref[:, x].astype(F32)
            buf[:, x] = total.astype(BF)
        copy_of(i).start()
    for i in range(parts):
        copy_of(i).wait()
    for copy in copies:
        copy.wait()


def corange_kernel(psi_ref, u_ref, state_in, out_ref, state_hbm, snap, acc, sem):
    del state_in
    samples, nx, ny, nz = u_ref.shape
    part = pl.ds(samples // 2, samples // 2)
    copy = pltpu.make_async_copy(u_ref.at[part], state_hbm.at[part], sem)
    copy.start()
    ranks = psi_ref.shape[2] // ROWS
    cols = ranks * ROWS
    for x in range(0, nx, 2):
        split_into(snap, x, u_ref[:, x])
        split_into(snap, x + 1, u_ref[:, x + 1])
        left = jnp.concatenate([side_by_side(snap, x), side_by_side(snap, x + 1)], axis=1)
        right = jnp.concatenate([side_by_side(psi_ref, x), side_by_side(psi_ref, x + 1)], axis=1)
        part = contract(left, right)
        acc[...] = part if x == 0 else acc[...] + part
    row = lax.broadcasted_iota(jnp.int32, (ROWS, cols), 0)
    col = lax.broadcasted_iota(jnp.int32, (ROWS, cols), 1) % ROWS
    fold = (
        lax.broadcasted_iota(jnp.int32, (cols, ranks), 0) // ROWS
        == lax.broadcasted_iota(jnp.int32, (cols, ranks), 1)
    ).astype(F32)
    picked = jnp.where((row == col)[None], acc[...].reshape(samples, ROWS, cols), 0.0).sum(1)
    out_ref[...] = jnp.dot(picked, fold, precision=lax.Precision.HIGHEST, preferred_element_type=F32)
    copy.wait()


def contract(left, right):
    return lax.dot_general(left, right, (((1,), (1,)), ((), ())), preferred_element_type=F32)


def corange_faces_kernel(
    main_ref, px, py, u_ref, cx0, cx1, cy0, cy1, hx0, hx1, hy0, hy1, out_ref, xbuf, ybuf
):
    samples, nx, ny, nz = u_ref.shape
    rows = flat(u_ref)
    for end, x, coef, halo in ((0, 0, cx0, hx0), (1, nx - 1, cx1, hx1)):
        xbuf[end] = coef[...] * (halo[...].astype(F32) - u_ref[:, x])
    for end, y, coef, halo in ((0, 0, cy0, hy0), (1, ny - 1, cy1, hy1)):
        for s in range(samples):
            ybuf[end, s] = coef[s] * (halo[s].astype(F32) - rows[y_line(u_ref, s, y), :])
    total = main_ref[...]
    for buf, psi in ((xbuf, px), (ybuf, py)):
        count = buf.shape[2]
        lines = buf.reshape(2 * samples * count, nz)
        for i in range(count):
            left = [
                lines[pl.ds(end * samples * count + i, samples, stride=count), :].astype(BF)
                for end in range(2)
            ]
            right = [psi[end, i] for end in range(2)]
            total = total + contract(jnp.concatenate(left, axis=1), jnp.concatenate(right, axis=1))
    out_ref[...] = total


def finish_kernel(*refs):
    w_ref, snap_ref = refs[-2:]
    edge_kernel(False, *refs[:-1])
    nx = w_ref.shape[1]

    def body(x, carry):
        split_into(snap_ref, x, w_ref[:, x])
        return carry

    lax.fori_loop(0, nx, body, 0)


def sum_kernel(*refs):
    total = refs[0][...]
    for ref in refs[1:-1]:
        total = total + ref[...]
    refs[-1][...] = total


def swap_pairs(count, parity, par):
    partner = {}
    for i in range(parity, count - 1, 2):
        partner[i] = i + 1
        partner[i + 1] = i
    pairs = []
    for i in range(count):
        for p in range(par):
            source = i * par + p
            if i in partner:
                pairs.append((source, partner[i] * par + p))
            else:
                pairs.append((source, i * par + (p + 1) % par))
    return pairs


ORDER = (("sy", 0), ("sy", 1), ("sx", 0), ("sx", 1))


def exchange(faces):
    ends = {"sx": faces[:2], "sy": faces[2:]}
    par = lax.axis_size("par")
    got = {}
    for axis, parity in ORDER:
        low, high = ends[axis]
        odd = lax.axis_index(axis) % 2 == 1
        mine = jnp.where(odd, high, low) if parity else jnp.where(odd, low, high)
        pairs = swap_pairs(lax.axis_size(axis), parity, par)
        got[axis, parity] = lax.ppermute(mine, (axis, "par"), pairs)
    halos = []
    for axis in ("sx", "sy"):
        index, count = lax.axis_index(axis), lax.axis_size(axis)
        odd = index % 2 == 1
        first, second = got[axis, 0], got[axis, 1]
        zero = jnp.zeros_like(first)
        halos.append(jnp.where(index == 0, zero, jnp.where(odd, first, second)))
        halos.append(jnp.where(index == count - 1, zero, jnp.where(odd, second, first)))
    return halos


def received(value, axis):
    count = lax.axis_size(axis)
    return [lax.ppermute(value, axis, [(i, i ^ shift) for i in range(count)]) for shift in range(1, count)]


def per_device(initial_state, conductivity, omega, psi, range_prev, corange_prev):
    samples, nx, ny, nz = block = initial_state.shape
    ranks = psi.shape[0]
    cells = samples * nx * ny * nz
    x_face, y_face = (samples, ny, nz), (samples, nx, nz)
    par = lax.axis_index("par")
    par_size = lax.axis_size("par")

    sent = vmem_call(
        faces_kernel,
        [((2,) + x_face, BF)] * 2 + [((2,) + y_face, BF)] * 2,
        "faces",
        scratch=[
            pltpu.VMEM((4,) + x_face, F32),
            pltpu.VMEM((4,) + y_face, F32),
            pltpu.SemaphoreType.DMA((8,)),
        ],
        hbm_in=(0, 1),
        flops=cells // 2,
        nbytes=cells,
    )(initial_state, conductivity)
    got = exchange(sent)
    halos = [g[1] for g in got]

    groups = samples // BLOCK
    state, moved, *made = vmem_call(
        first_kernel,
        [(block, F32)] * 6 + [(x_face, F32)] * 2 + [(y_face, F32)] * 2,
        "first",
        limit=7 << 20,
        scratch=[pltpu.VMEM(block, F32), pltpu.SemaphoreType.DMA((2, groups))],
        hbm_in=(0, 1),
        flops=36 * cells,
        nbytes=16 * cells,
    )(initial_state, conductivity)
    coefs, kfaces = made[:4], made[4:]
    face_coefs = [k + HALF * g[0].astype(F32) for k, g in zip(kfaces, got)]

    own_ranks = range_prev.shape[0]
    own_cols = lax.dynamic_slice_in_dim(omega, par * own_ranks, own_ranks, 1).T
    source = (par + par_size - 1) % par_size
    omega_blocks = jnp.stack(
        [lax.dynamic_slice_in_dim(own_cols, p * samples, samples, 1) for p in (par, source)]
    )
    held_psi, psi_y = vmem_call(
        psi_kernel,
        [(split_shape(psi.shape), BF), ((2, nx, ranks, nz), BF)],
        "psi",
        limit=6 << 20,
        scratch=[
            pltpu.VMEM(psi.shape, BF),
            pltpu.VMEM((ranks, ny, nz), F32),
            pltpu.SemaphoreType.DMA((4,)),
        ],
        hbm_in=(0,),
        flops=4 * cells,
        nbytes=4 * cells,
    )(psi)
    kept = (held_psi, psi_y)
    for step in range(STEPS):
        if step > 0:
            halos = exchange(edges)
            last = step == STEPS - 1
            moved, *written = vmem_call(
                last_step_kernel if last else step_kernel,
                [(block, F32)] * (2 if last else 1),
                "step",
                scratch=[pltpu.SemaphoreType.DMA((groups,))] if last else [],
                hbm_out=(1,),
                flops=24 * cells,
                nbytes=8 * cells,
            )(state, *coefs, *kept)
        if step == 2:
            psi_x, weights, prev = vmem_call(
                lines_kernel,
                [
                    ((2, ny, ranks, nz), BF),
                    ((2, own_ranks * ROWS, samples * ROWS), BF),
                    (range_prev.shape, BF),
                ],
                "lines",
                limit=4 << 20,
                scratch=[
                    pltpu.VMEM((2, ranks, ny, nz), BF),
                    pltpu.VMEM((ranks, ny, nz), F32),
                    pltpu.SemaphoreType.DMA((3,)),
                ],
                hbm_in=(0, 1),
                flops=cells,
                nbytes=cells,
            )(psi, range_prev, omega_blocks, moved)
            kept += (psi_x, weights, prev)
        if step < STEPS - 1:
            state, *edges = vmem_call(
                functools.partial(edge_kernel, True),
                [(block, F32), (x_face, BF), (x_face, BF), (y_face, BF), (y_face, BF)],
                "edge",
                aliases={0: 0},
                flops=cells,
                nbytes=cells,
            )(moved, state, *face_coefs, *halos, *kept)

    main, written = vmem_call(
        corange_kernel,
        [((samples, ranks), F32), (block, F32)],
        "corange",
        limit=6 << 20,
        scratch=[
            pltpu.VMEM(split_shape(block), BF),
            pltpu.VMEM((samples * ROWS, ranks * ROWS), F32),
            pltpu.SemaphoreType.DMA,
        ],
        hbm_in=(2,),
        hbm_out=(1,),
        aliases={2: 1},
        flops=2 * ranks * ROWS * cells,
        nbytes=4 * cells,
    )(held_psi, moved, *written)
    partial_sum = vmem_call(
        corange_faces_kernel,
        [((samples, ranks), F32)],
        "corange_faces",
        scratch=[pltpu.VMEM((2,) + x_face, F32), pltpu.VMEM((2,) + y_face, F32)],
        flops=cells,
        nbytes=cells,
    )(main, psi_x, psi_y, state, *face_coefs, *halos)[0]
    first_sums = received(partial_sum, "sx")
    final, snapshot = vmem_call(
        finish_kernel,
        [(block, F32), (split_shape(block), BF)],
        "finish",
        aliases={0: 0},
        flops=cells,
        nbytes=2 * cells,
    )(moved, state, *face_coefs, *halos, prev, weights, partial_sum)
    other = lax.ppermute(snapshot, "par", [(i, (i + 1) % par_size) for i in range(par_size)])
    range_sketch, final_state, done = vmem_call(
        range_kernel,
        [(range_prev.shape, BF), (block, F32), ((samples, ranks), F32)],
        "range",
        limit=6 << 20,
        scratch=[pltpu.VMEM(range_prev.shape, BF), pltpu.SemaphoreType.DMA((2, 4))],
        hbm_in=(5,),
        hbm_out=(0, 1),
        aliases={5: 1},
        flops=2 * ranks * ROWS * cells,
        nbytes=4 * cells,
    )(weights, snapshot, other, prev, final, written)
    line_sum = vmem_call(
        sum_kernel, [((samples, ranks), F32)], "line_sum", flops=SUM_COST, nbytes=SUM_COST
    )(partial_sum, *first_sums)[0]
    corange = sum(received(line_sum, "sy"), corange_prev.T + line_sum) + done
    return final_state, range_sketch, corange.T


def solution(mesh):
    in_specs = (
        P("par", "sx", "sy", None),
        P("par", "sx", "sy", None),
        P(),
        P(None, "sx", "sy", None),
        P("par", "sx", "sy", None),
        P(None, "par"),
    )
    out_specs = (P("par", "sx", "sy", None), P("par", "sx", "sy", None), P(None, "par"))
    return jax.shard_map(
        per_device, mesh=mesh, in_specs=in_specs, out_specs=out_specs, check_vma=False
    )
```

```python
import functools

import jax
import jax.numpy as jnp
from jax import lax
from jax.experimental import pallas as pl
from jax.experimental.pallas import tpu as pltpu
from jax.sharding import PartitionSpec as P

STEPS = 4
BF = jnp.bfloat16
F32 = jnp.float32
HALF = 0.16 * 0.5
BLOCK = 8
ROWS = 8
SUM_COST = 20 << 20


def vmem_call(
    kernel, outs, name, limit=3 << 20, scratch=(), hbm_in=(), hbm_out=(), aliases=None, flops=0, nbytes=0
):
    def call(*args):
        in_specs = []
        ready = []
        for i, arg in enumerate(args):
            in_specs.append(pl.BlockSpec(memory_space=pltpu.HBM if i in hbm_in else pltpu.VMEM))
            ready.append(
                pltpu.with_memory_space_constraint(arg, pltpu.HBM if i in hbm_in else pltpu.VMEM)
            )
        out_shape = []
        out_specs = []
        for i, (shape, dtype) in enumerate(outs):
            out_shape.append((pltpu.HBM if i in hbm_out else pltpu.VMEM)(shape, dtype))
            out_specs.append(pl.BlockSpec(memory_space=pltpu.HBM if i in hbm_out else pltpu.VMEM))
        return pl.pallas_call(
            kernel,
            out_shape=out_shape,
            in_specs=in_specs,
            out_specs=out_specs,
            scratch_shapes=list(scratch),
            input_output_aliases=aliases or {},
            name=name,
            compiler_params=pltpu.CompilerParams(vmem_limit_bytes=limit),
            cost_estimate=pl.CostEstimate(flops=flops, bytes_accessed=nbytes, transcendentals=0),
        )(*ready)

    return call


def faces_kernel(u_ref, k_ref, lx, ux, ly, uy, xbuf, ybuf, sem):
    _, nx, ny, _ = u_ref.shape
    copies = []
    for i, (ref, end) in enumerate(((k_ref, 0), (u_ref, 0), (k_ref, 1), (u_ref, 1))):
        x, y = end * (nx - 1), end * (ny - 1)
        copies.append(pltpu.make_async_copy(ref.at[:, x], xbuf.at[i], sem.at[i]))
        copies.append(pltpu.make_async_copy(ref.at[:, :, y], ybuf.at[i], sem.at[4 + i]))
    for copy in copies:
        copy.start()
    for i in range(4):
        copies[2 * i].wait()
        copies[2 * i + 1].wait()
        (lx if i < 2 else ux)[i % 2] = xbuf[i].astype(BF)
        (ly if i < 2 else uy)[i % 2] = ybuf[i].astype(BF)


def y_line(ref, s, y):
    _, nx, ny, _ = ref.shape
    return pl.ds(s * (nx * ny) + y, nx, stride=ny)


def flat(ref):
    samples, nx, ny, nz = ref.shape
    return ref.reshape(samples * nx * ny, nz)


def first_kernel(
    u_hbm, k_hbm, u_ref, w_ref, cx_ref, cy_ref, cup_ref, cdown_ref, kx0, kx1, ky0, ky1, buf, sem
):
    samples, nx, ny, nz = u_ref.shape
    shape = (BLOCK, ny, nz)
    groups = samples // BLOCK
    y_open = lax.broadcasted_iota(jnp.int32, shape, 1) < ny - 1
    lane = lax.broadcasted_iota(jnp.int32, shape, 2)
    rows = flat(buf)

    def copies(g):
        part = pl.ds(g * BLOCK, BLOCK)
        return (
            pltpu.make_async_copy(k_hbm.at[part], buf.at[part], sem.at[0, g]),
            pltpu.make_async_copy(u_hbm.at[part], u_ref.at[part], sem.at[1, g]),
        )

    for g in range(groups):
        for copy in copies(g):
            copy.start()

    def before(g):
        for copy in copies(g):
            copy.wait()
        part = pl.ds(g * BLOCK, BLOCK)
        for i in range(BLOCK):
            s = g * BLOCK + i
            ky0[s] = rows[y_line(buf, s, 0), :] * HALF
            ky1[s] = rows[y_line(buf, s, ny - 1), :] * HALF
        k = buf[part, 0] * HALF
        kx0[part] = k
        for x in range(nx):
            if x + 1 < nx:
                k_next = buf[part, x + 1] * HALF
                cx_ref[part, x] = k + k_next
            cy_ref[part, x] = jnp.where(y_open, k + pltpu.roll(k, ny - 1, 1), 0.0)
            cup_ref[part, x] = k + jnp.where(lane < nz - 1, pltpu.roll(k, nz - 1, 2), 0.0)
            cdown_ref[part, x] = k + jnp.where(lane > 0, pltpu.roll(k, 1, 2), 0.0)
            if x + 1 < nx:
                k = k_next
        kx1[part] = k

    step_body(u_ref, cx_ref, cy_ref, cup_ref, cdown_ref, w_ref, before)


def difference_matrix(nz):
    row = lax.broadcasted_iota(jnp.int32, (nz, nz), 0)
    col = lax.broadcasted_iota(jnp.int32, (nz, nz), 1)
    eye = (row == col).astype(F32)
    up = (row == col + 1).astype(F32) - eye
    down = (row + 1 == col).astype(F32) - eye
    both = jnp.concatenate([up, down], axis=1).astype(BF)
    return jnp.concatenate([both, both], axis=0)


def step_kernel(u_ref, cx_ref, cy_ref, cup_ref, cdown_ref, *refs):
    step_body(u_ref, cx_ref, cy_ref, cup_ref, cdown_ref, refs[-1])


def last_step_kernel(u_ref, cx_ref, cy_ref, cup_ref, cdown_ref, *refs):
    w_ref, state_hbm, sem = refs[-3:]
    half = u_ref.shape[0] // BLOCK // 2

    def copy_of(g):
        part = pl.ds(g * BLOCK, BLOCK)
        return pltpu.make_async_copy(w_ref.at[part], state_hbm.at[part], sem.at[g])

    def after(g):
        @pl.when(g < half)
        def _():
            copy_of(g).start()

    step_body(u_ref, cx_ref, cy_ref, cup_ref, cdown_ref, w_ref, after=after)
    for g in range(half):
        copy_of(g).wait()


def step_body(u_ref, cx_ref, cy_ref, cup_ref, cdown_ref, w_ref, before=None, after=None):
    samples, nx, ny, nz = u_ref.shape
    shape = (BLOCK, ny, nz)
    matrix = difference_matrix(nz)

    def body(g, carry):
        if before:
            before(g)
        part = pl.ds(g * BLOCK, BLOCK)
        u = u_ref[part, 0]
        for x in range(nx):
            total = u
            if x + 1 < nx:
                u_next = u_ref[part, x + 1]
                flux = cx_ref[part, x] * (u_next - u)
                total = total + flux
            if x > 0:
                total = total - flux_low
            fy = cy_ref[part, x] * (pltpu.roll(u, ny - 1, 1) - u)
            total = total + (fy - pltpu.roll(fy, 1, 1))
            wide = u.reshape(BLOCK * ny, nz)
            coarse = wide.astype(BF)
            fine = (wide - coarse.astype(F32)).astype(BF)
            dz = jnp.dot(jnp.concatenate([coarse, fine], axis=1), matrix, preferred_element_type=F32)
            total = total + cup_ref[part, x] * dz[:, :nz].reshape(shape)
            total = total + cdown_ref[part, x] * dz[:, nz:].reshape(shape)
            w_ref[part, x] = total
            if x + 1 < nx:
                u, flux_low = u_next, flux
        if after:
            after(g)
        return carry

    lax.fori_loop(0, samples // BLOCK, body, 0)


def edge_kernel(lined, w_in, u_ref, *refs):
    del w_in
    cx0, cx1, cy0, cy1, hx0, hx1, hy0, hy1 = refs[:8]
    w_ref, lx, ux, ly, uy, *lines = refs[-7:]
    samples, nx, ny, nz = u_ref.shape
    w_rows, u_rows = flat(w_ref), flat(u_ref)

    def one(s):
        for x, coef, halo in ((0, cx0, hx0), (nx - 1, cx1, hx1)):
            w_ref[s, x] = w_ref[s, x] + coef[s] * (halo[s].astype(F32) - u_ref[s, x])
        for end, (coef, halo, out) in enumerate(((cy0, hy0, ly), (cy1, hy1, uy))):
            line = y_line(u_ref, s, end * (ny - 1))
            state = refs[8 + end][s] if lined else u_rows[line, :]
            value = w_rows[line, :] + coef[s] * (halo[s].astype(F32) - state)
            w_rows[line, :] = value
            out[s] = value.astype(BF)
            lines[end][s] = value
        lx[s] = w_ref[s, 0].astype(BF)
        ux[s] = w_ref[s, nx - 1].astype(BF)

    def body(i, carry):
        for j in range(4):
            one(i * 4 + j)
        return carry

    lax.fori_loop(0, samples // 4, body, 0)


def split_shape(shape):
    count, nx, ny, nz = shape
    return (nx, ny // ROWS, count * ROWS, nz)


def split_into(out_ref, x, value):
    count, ny, nz = value.shape
    for h in range(ny // ROWS):
        part = value[:, h * ROWS : (h + 1) * ROWS]
        out_ref[x, h] = part.reshape(count * ROWS, nz).astype(BF)


def one_hot(rows, cols, row_width, col_width):
    row = lax.broadcasted_iota(jnp.int32, (rows, cols), 0) // row_width
    col = lax.broadcasted_iota(jnp.int32, (rows, cols), 1) // col_width
    return (row == col).astype(BF)


def spread(block):
    rows, cols = block.shape
    tall = jnp.dot(one_hot(rows * ROWS, rows, ROWS, 1), block, preferred_element_type=F32).astype(BF)
    full = jnp.dot(tall, one_hot(cols, cols * ROWS, 1, ROWS), preferred_element_type=F32)
    row = lax.broadcasted_iota(jnp.int32, full.shape, 0) % ROWS
    col = lax.broadcasted_iota(jnp.int32, full.shape, 1) % ROWS
    return jnp.where(row == col, full, 0.0).astype(BF)


def lines_kernel(psi_hbm, prev_hbm, omega_ref, after, x_ref, weight_ref, prev_ref, xbuf, wide, sem):
    del after
    ranks, nx, ny, nz = psi_hbm.shape
    rows = wide.reshape(ranks * ny, nz)
    copies = []
    for end in range(2):
        copies.append(
            pltpu.make_async_copy(psi_hbm.at[:, end * (nx - 1)], xbuf.at[end], sem.at[end])
        )
    copies.append(pltpu.make_async_copy(prev_hbm, prev_ref, sem.at[2]))
    for copy in copies:
        copy.start()
    for i in range(omega_ref.shape[0]):
        weight_ref[i] = spread(omega_ref[i])
    for end in range(2):
        copies[end].wait()
        wide[...] = xbuf[end].astype(F32)
        for y in range(ny):
            x_ref[end, y] = rows[pl.ds(y, ranks, stride=ny), :].astype(BF)
    copies[2].wait()


def psi_kernel(psi_hbm, out_ref, y_ref, buf, wide, sem):
    ranks, nx, ny, nz = psi_hbm.shape
    parts = 4
    rows = wide.reshape(ranks * ny, nz)

    def copy_of(i):
        part = pl.ds(i * (nx // parts), nx // parts)
        return pltpu.make_async_copy(psi_hbm.at[:, part], buf.at[:, part], sem.at[i])

    for i in range(parts):
        copy_of(i).start()

    def body(x, carry):
        value = buf[:, x].astype(F32)
        split_into(out_ref, x, value)
        wide[...] = value
        for end in range(2):
            y_ref[end, x] = rows[pl.ds(end * (ny - 1), ranks, stride=ny), :].astype(BF)
        return carry

    for i in range(parts):
        copy_of(i).wait()
        lax.fori_loop(i * (nx // parts), (i + 1) * (nx // parts), body, 0)


def side_by_side(ref, x):
    return jnp.concatenate([ref[x, h] for h in range(ref.shape[1])], axis=1)


def range_kernel(
    weight_ref, own_ref, other_ref, prev_ref, u_ref, state_in, out_ref, state_hbm, done_ref, buf, sem
):
    del state_in
    ranks, nx, ny, nz = prev_ref.shape
    parts = 4
    inner = pl.ds(1, nx - 2)
    copies = []
    for i, (x, y) in enumerate(((0, 0), (nx - 1, ny - 1))):
        copies.append(pltpu.make_async_copy(u_ref.at[:, x], state_hbm.at[:, x], sem.at[1, i]))
        copies.append(
            pltpu.make_async_copy(u_ref.at[:, inner, y], state_hbm.at[:, inner, y], sem.at[1, 2 + i])
        )
    for copy in copies:
        copy.start()
    done_ref[...] = jnp.zeros_like(done_ref)

    def copy_of(i):
        part = pl.ds(i * (nx // parts), nx // parts)
        return pltpu.make_async_copy(buf.at[:, part], out_ref.at[:, part], sem.at[0, i])

    for i in range(parts):
        for x in range(i * (nx // parts), (i + 1) * (nx // parts)):
            value = jnp.dot(weight_ref[0], side_by_side(own_ref, x), preferred_element_type=F32)
            value += jnp.dot(weight_ref[1], side_by_side(other_ref, x), preferred_element_type=F32)
            halves = [
                value[:, h * nz : (h + 1) * nz].reshape(ranks, ROWS, nz) for h in range(ny // ROWS)
            ]
            total = jnp.concatenate(halves, axis=1) + prev_ref[:, x].astype(F32)
            buf[:, x] = total.astype(BF)
        copy_of(i).start()
    for i in range(parts):
        copy_of(i).wait()
    for copy in copies:
        copy.wait()


def corange_kernel(psi_ref, u_ref, state_in, out_ref, state_hbm, snap, acc, sem):
    del state_in
    samples, nx, ny, nz = u_ref.shape
    part = pl.ds(samples // 2, samples // 2)
    copy = pltpu.make_async_copy(u_ref.at[part], state_hbm.at[part], sem)
    copy.start()
    ranks = psi_ref.shape[2] // ROWS
    cols = ranks * ROWS
    for x in range(0, nx, 2):
        split_into(snap, x, u_ref[:, x])
        split_into(snap, x + 1, u_ref[:, x + 1])
        left = jnp.concatenate([side_by_side(snap, x), side_by_side(snap, x + 1)], axis=1)
        right = jnp.concatenate([side_by_side(psi_ref, x), side_by_side(psi_ref, x + 1)], axis=1)
        part = contract(left, right)
        acc[...] = part if x == 0 else acc[...] + part
    row = lax.broadcasted_iota(jnp.int32, (ROWS, cols), 0)
    col = lax.broadcasted_iota(jnp.int32, (ROWS, cols), 1) % ROWS
    fold = (
        lax.broadcasted_iota(jnp.int32, (cols, ranks), 0) // ROWS
        == lax.broadcasted_iota(jnp.int32, (cols, ranks), 1)
    ).astype(F32)
    picked = jnp.where((row == col)[None], acc[...].reshape(samples, ROWS, cols), 0.0).sum(1)
    out_ref[...] = jnp.dot(picked, fold, precision=lax.Precision.HIGHEST, preferred_element_type=F32)
    copy.wait()


def contract(left, right):
    return lax.dot_general(left, right, (((1,), (1,)), ((), ())), preferred_element_type=F32)


def finish_kernel(w_in, u_ref, cx0, cx1, cy0, cy1, hx0, hx1, hy0, hy1, *refs):
    del w_in
    ends, (main_ref, px, py) = refs[:2], refs[2:5]
    w_ref, out_ref, snap_ref, xbuf, ybuf = refs[-5:]
    samples, nx, ny, nz = u_ref.shape
    w_rows = flat(w_ref)

    def one(s):
        for end, (coef, halo) in enumerate(((cx0, hx0), (cx1, hx1))):
            x = end * (nx - 1)
            flux = coef[s] * (halo[s].astype(F32) - u_ref[s, x])
            xbuf[end, s] = flux
            w_ref[s, x] = w_ref[s, x] + flux
        for end, (coef, halo) in enumerate(((cy0, hy0), (cy1, hy1))):
            line = y_line(u_ref, s, end * (ny - 1))
            flux = coef[s] * (halo[s].astype(F32) - ends[end][s])
            ybuf[end, s] = flux
            w_rows[line, :] = w_rows[line, :] + flux

    def patch(i, carry):
        for j in range(4):
            one(i * 4 + j)
        return carry

    lax.fori_loop(0, samples // 4, patch, 0)
    total = main_ref[...]
    for buf, psi in ((xbuf, px), (ybuf, py)):
        count = buf.shape[2]
        lines = buf.reshape(2 * samples * count, nz)
        for i in range(count):
            left = [
                lines[pl.ds(end * samples * count + i, samples, stride=count), :].astype(BF)
                for end in range(2)
            ]
            right = [psi[end, i] for end in range(2)]
            total = total + contract(jnp.concatenate(left, axis=1), jnp.concatenate(right, axis=1))
    out_ref[...] = total

    def body(x, carry):
        split_into(snap_ref, x, w_ref[:, x])
        return carry

    lax.fori_loop(0, nx, body, 0)


def sum_kernel(*refs):
    total = refs[0][...]
    for ref in refs[1:-1]:
        total = total + ref[...]
    refs[-1][...] = total


def swap_pairs(count, parity, par):
    partner = {}
    for i in range(parity, count - 1, 2):
        partner[i] = i + 1
        partner[i + 1] = i
    pairs = []
    for i in range(count):
        for p in range(par):
            source = i * par + p
            if i in partner:
                pairs.append((source, partner[i] * par + p))
            else:
                pairs.append((source, i * par + (p + 1) % par))
    return pairs


ORDER = (("sy", 0), ("sy", 1), ("sx", 0), ("sx", 1))


def exchange(faces):
    ends = {"sx": faces[:2], "sy": faces[2:]}
    par = lax.axis_size("par")
    got = {}
    for axis, parity in ORDER:
        low, high = ends[axis]
        odd = lax.axis_index(axis) % 2 == 1
        mine = jnp.where(odd, high, low) if parity else jnp.where(odd, low, high)
        pairs = swap_pairs(lax.axis_size(axis), parity, par)
        got[axis, parity] = lax.ppermute(mine, (axis, "par"), pairs)
    halos = []
    for axis in ("sx", "sy"):
        index, count = lax.axis_index(axis), lax.axis_size(axis)
        odd = index % 2 == 1
        first, second = got[axis, 0], got[axis, 1]
        zero = jnp.zeros_like(first)
        halos.append(jnp.where(index == 0, zero, jnp.where(odd, first, second)))
        halos.append(jnp.where(index == count - 1, zero, jnp.where(odd, second, first)))
    return halos


def received(value, axis):
    count = lax.axis_size(axis)
    return [lax.ppermute(value, axis, [(i, i ^ shift) for i in range(count)]) for shift in range(1, count)]


def per_device(initial_state, conductivity, omega, psi, range_prev, corange_prev):
    samples, nx, ny, nz = block = initial_state.shape
    ranks = psi.shape[0]
    cells = samples * nx * ny * nz
    x_face, y_face = (samples, ny, nz), (samples, nx, nz)
    par = lax.axis_index("par")
    par_size = lax.axis_size("par")

    sent = vmem_call(
        faces_kernel,
        [((2,) + x_face, BF)] * 2 + [((2,) + y_face, BF)] * 2,
        "faces",
        scratch=[
            pltpu.VMEM((4,) + x_face, F32),
            pltpu.VMEM((4,) + y_face, F32),
            pltpu.SemaphoreType.DMA((8,)),
        ],
        hbm_in=(0, 1),
        flops=cells // 2,
        nbytes=cells,
    )(initial_state, conductivity)
    got = exchange(sent)
    halos = [g[1] for g in got]

    groups = samples // BLOCK
    state, moved, *made = vmem_call(
        first_kernel,
        [(block, F32)] * 6 + [(x_face, F32)] * 2 + [(y_face, F32)] * 2,
        "first",
        limit=7 << 20,
        scratch=[pltpu.VMEM(block, F32), pltpu.SemaphoreType.DMA((2, groups))],
        hbm_in=(0, 1),
        flops=36 * cells,
        nbytes=16 * cells,
    )(initial_state, conductivity)
    coefs, kfaces = made[:4], made[4:]
    face_coefs = [k + HALF * g[0].astype(F32) for k, g in zip(kfaces, got)]

    own_ranks = range_prev.shape[0]
    own_cols = lax.dynamic_slice_in_dim(omega, par * own_ranks, own_ranks, 1).T
    source = (par + par_size - 1) % par_size
    omega_blocks = jnp.stack(
        [lax.dynamic_slice_in_dim(own_cols, p * samples, samples, 1) for p in (par, source)]
    )
    held_psi, psi_y = vmem_call(
        psi_kernel,
        [(split_shape(psi.shape), BF), ((2, nx, ranks, nz), BF)],
        "psi",
        limit=6 << 20,
        scratch=[
            pltpu.VMEM(psi.shape, BF),
            pltpu.VMEM((ranks, ny, nz), F32),
            pltpu.SemaphoreType.DMA((4,)),
        ],
        hbm_in=(0,),
        flops=4 * cells,
        nbytes=4 * cells,
    )(psi)
    kept = (held_psi, psi_y)
    lines = []
    for step in range(STEPS):
        if step > 0:
            halos = exchange(edges)
            last = step == STEPS - 1
            moved, *written = vmem_call(
                last_step_kernel if last else step_kernel,
                [(block, F32)] * (2 if last else 1),
                "step",
                scratch=[pltpu.SemaphoreType.DMA((groups,))] if last else [],
                hbm_out=(1,),
                flops=24 * cells,
                nbytes=8 * cells,
            )(state, *coefs, *kept)
        if step == 2:
            psi_x, weights, prev = vmem_call(
                lines_kernel,
                [
                    ((2, ny, ranks, nz), BF),
                    ((2, own_ranks * ROWS, samples * ROWS), BF),
                    (range_prev.shape, BF),
                ],
                "lines",
                limit=4 << 20,
                scratch=[
                    pltpu.VMEM((2, ranks, ny, nz), BF),
                    pltpu.VMEM((ranks, ny, nz), F32),
                    pltpu.SemaphoreType.DMA((3,)),
                ],
                hbm_in=(0, 1),
                flops=cells,
                nbytes=cells,
            )(psi, range_prev, omega_blocks, moved)
            kept += (psi_x, weights, prev)
        if step < STEPS - 1:
            outs = [(block, F32)] + [(x_face, BF)] * 2 + [(y_face, BF)] * 2 + [(y_face, F32)] * 2
            state, *edges = vmem_call(
                functools.partial(edge_kernel, step > 0),
                outs,
                "edge",
                aliases={0: 0},
                flops=cells,
                nbytes=cells,
            )(moved, state, *face_coefs, *halos, *lines, *kept)
            edges, lines = edges[:4], edges[4:]

    main, written = vmem_call(
        corange_kernel,
        [((samples, ranks), F32), (block, F32)],
        "corange",
        limit=6 << 20,
        scratch=[
            pltpu.VMEM(split_shape(block), BF),
            pltpu.VMEM((samples * ROWS, ranks * ROWS), F32),
            pltpu.SemaphoreType.DMA,
        ],
        hbm_in=(2,),
        hbm_out=(1,),
        aliases={2: 1},
        flops=2 * ranks * ROWS * cells,
        nbytes=4 * cells,
    )(held_psi, moved, *written)
    final, partial_sum, snapshot = vmem_call(
        finish_kernel,
        [(block, F32), ((samples, ranks), F32), (split_shape(block), BF)],
        "finish",
        scratch=[pltpu.VMEM((2,) + x_face, F32), pltpu.VMEM((2,) + y_face, F32)],
        aliases={0: 0},
        flops=cells,
        nbytes=2 * cells,
    )(moved, state, *face_coefs, *halos, *lines, main, psi_x, psi_y, prev, weights)
    first_sums = received(partial_sum, "sx")
    other = lax.ppermute(snapshot, "par", [(i, (i + 1) % par_size) for i in range(par_size)])
    range_sketch, final_state, done = vmem_call(
        range_kernel,
        [(range_prev.shape, BF), (block, F32), ((samples, ranks), F32)],
        "range",
        limit=6 << 20,
        scratch=[pltpu.VMEM(range_prev.shape, BF), pltpu.SemaphoreType.DMA((2, 4))],
        hbm_in=(5,),
        hbm_out=(0, 1),
        aliases={5: 1},
        flops=2 * ranks * ROWS * cells,
        nbytes=4 * cells,
    )(weights, snapshot, other, prev, final, written)
    line_sum = vmem_call(
        sum_kernel, [((samples, ranks), F32)], "line_sum", flops=SUM_COST, nbytes=SUM_COST
    )(partial_sum, *first_sums)[0]
    corange = sum(received(line_sum, "sy"), corange_prev.T + line_sum) + done
    return final_state, range_sketch, corange.T


def solution(mesh):
    in_specs = (
        P("par", "sx", "sy", None),
        P("par", "sx", "sy", None),
        P(),
        P(None, "sx", "sy", None),
        P("par", "sx", "sy", None),
        P(None, "par"),
    )
    out_specs = (P("par", "sx", "sy", None), P("par", "sx", "sy", None), P(None, "par"))
    return jax.shard_map(
        per_device, mesh=mesh, in_specs=in_specs, out_specs=out_specs, check_vma=False
    )
```

```python
import functools

import jax
import jax.numpy as jnp
from jax import lax
from jax.experimental import pallas as pl
from jax.experimental.pallas import tpu as pltpu
from jax.sharding import PartitionSpec as P

STEPS = 4
BF = jnp.bfloat16
F32 = jnp.float32
HALF = 0.16 * 0.5
BLOCK = 8
ROWS = 8
SUM_COST = 20 << 20


def vmem_call(
    kernel, outs, name, limit=3 << 20, scratch=(), hbm_in=(), hbm_out=(), aliases=None, flops=0, nbytes=0
):
    def call(*args):
        in_specs = []
        ready = []
        for i, arg in enumerate(args):
            in_specs.append(pl.BlockSpec(memory_space=pltpu.HBM if i in hbm_in else pltpu.VMEM))
            ready.append(
                pltpu.with_memory_space_constraint(arg, pltpu.HBM if i in hbm_in else pltpu.VMEM)
            )
        out_shape = []
        out_specs = []
        for i, (shape, dtype) in enumerate(outs):
            out_shape.append((pltpu.HBM if i in hbm_out else pltpu.VMEM)(shape, dtype))
            out_specs.append(pl.BlockSpec(memory_space=pltpu.HBM if i in hbm_out else pltpu.VMEM))
        return pl.pallas_call(
            kernel,
            out_shape=out_shape,
            in_specs=in_specs,
            out_specs=out_specs,
            scratch_shapes=list(scratch),
            input_output_aliases=aliases or {},
            name=name,
            compiler_params=pltpu.CompilerParams(vmem_limit_bytes=limit),
            cost_estimate=pl.CostEstimate(flops=flops, bytes_accessed=nbytes, transcendentals=0),
        )(*ready)

    return call


def faces_kernel(u_ref, k_ref, lx, ux, ly, uy, xbuf, ybuf, sem):
    _, nx, ny, _ = u_ref.shape
    copies = []
    for i, (ref, end) in enumerate(((k_ref, 0), (u_ref, 0), (k_ref, 1), (u_ref, 1))):
        x, y = end * (nx - 1), end * (ny - 1)
        copies.append(pltpu.make_async_copy(ref.at[:, x], xbuf.at[i], sem.at[i]))
        copies.append(pltpu.make_async_copy(ref.at[:, :, y], ybuf.at[i], sem.at[4 + i]))
    for copy in copies:
        copy.start()
    for i in range(4):
        copies[2 * i].wait()
        copies[2 * i + 1].wait()
        (lx if i < 2 else ux)[i % 2] = xbuf[i].astype(BF)
        (ly if i < 2 else uy)[i % 2] = ybuf[i].astype(BF)


def y_line(ref, s, y):
    _, nx, ny, _ = ref.shape
    return pl.ds(s * (nx * ny) + y, nx, stride=ny)


def flat(ref):
    samples, nx, ny, nz = ref.shape
    return ref.reshape(samples * nx * ny, nz)


def first_kernel(
    u_hbm, k_hbm, u_ref, w_ref, cx_ref, cy_ref, cup_ref, cdown_ref, kx0, kx1, ky0, ky1, buf, sem
):
    samples, nx, ny, nz = u_ref.shape
    shape = (BLOCK, ny, nz)
    groups = samples // BLOCK
    y_open = lax.broadcasted_iota(jnp.int32, shape, 1) < ny - 1
    lane = lax.broadcasted_iota(jnp.int32, shape, 2)
    rows = flat(buf)

    def copies(g):
        part = pl.ds(g * BLOCK, BLOCK)
        return (
            pltpu.make_async_copy(k_hbm.at[part], buf.at[part], sem.at[0, g]),
            pltpu.make_async_copy(u_hbm.at[part], u_ref.at[part], sem.at[1, g]),
        )

    for g in range(groups):
        for copy in copies(g):
            copy.start()

    def before(g):
        for copy in copies(g):
            copy.wait()
        part = pl.ds(g * BLOCK, BLOCK)
        for i in range(BLOCK):
            s = g * BLOCK + i
            ky0[s] = rows[y_line(buf, s, 0), :] * HALF
            ky1[s] = rows[y_line(buf, s, ny - 1), :] * HALF
        k = buf[part, 0] * HALF
        kx0[part] = k
        for x in range(nx):
            if x + 1 < nx:
                k_next = buf[part, x + 1] * HALF
                cx_ref[part, x] = k + k_next
            cy_ref[part, x] = jnp.where(y_open, k + pltpu.roll(k, ny - 1, 1), 0.0)
            cup_ref[part, x] = k + jnp.where(lane < nz - 1, pltpu.roll(k, nz - 1, 2), 0.0)
            cdown_ref[part, x] = k + jnp.where(lane > 0, pltpu.roll(k, 1, 2), 0.0)
            if x + 1 < nx:
                k = k_next
        kx1[part] = k

    step_body(u_ref, cx_ref, cy_ref, cup_ref, cdown_ref, w_ref, before)


def difference_matrix(nz):
    row = lax.broadcasted_iota(jnp.int32, (nz, nz), 0)
    col = lax.broadcasted_iota(jnp.int32, (nz, nz), 1)
    eye = (row == col).astype(F32)
    up = (row == col + 1).astype(F32) - eye
    down = (row + 1 == col).astype(F32) - eye
    both = jnp.concatenate([up, down], axis=1).astype(BF)
    return jnp.concatenate([both, both], axis=0)


def step_kernel(u_ref, cx_ref, cy_ref, cup_ref, cdown_ref, *refs):
    step_body(u_ref, cx_ref, cy_ref, cup_ref, cdown_ref, refs[-1])


def last_step_kernel(u_ref, cx_ref, cy_ref, cup_ref, cdown_ref, *refs):
    w_ref, state_hbm, sem = refs[-3:]
    half = u_ref.shape[0] // BLOCK // 2

    def copy_of(g):
        part = pl.ds(g * BLOCK, BLOCK)
        return pltpu.make_async_copy(w_ref.at[part], state_hbm.at[part], sem.at[g])

    def after(g):
        @pl.when(g < half)
        def _():
            copy_of(g).start()

    step_body(u_ref, cx_ref, cy_ref, cup_ref, cdown_ref, w_ref, after=after)
    for g in range(half):
        copy_of(g).wait()


def step_body(u_ref, cx_ref, cy_ref, cup_ref, cdown_ref, w_ref, before=None, after=None):
    samples, nx, ny, nz = u_ref.shape
    shape = (BLOCK, ny, nz)
    matrix = difference_matrix(nz)

    def body(g, carry):
        if before:
            before(g)
        part = pl.ds(g * BLOCK, BLOCK)
        u = u_ref[part, 0]
        for x in range(nx):
            total = u
            if x + 1 < nx:
                u_next = u_ref[part, x + 1]
                flux = cx_ref[part, x] * (u_next - u)
                total = total + flux
            if x > 0:
                total = total - flux_low
            fy = cy_ref[part, x] * (pltpu.roll(u, ny - 1, 1) - u)
            total = total + (fy - pltpu.roll(fy, 1, 1))
            wide = u.reshape(BLOCK * ny, nz)
            coarse = wide.astype(BF)
            fine = (wide - coarse.astype(F32)).astype(BF)
            dz = jnp.dot(jnp.concatenate([coarse, fine], axis=1), matrix, preferred_element_type=F32)
            total = total + cup_ref[part, x] * dz[:, :nz].reshape(shape)
            total = total + cdown_ref[part, x] * dz[:, nz:].reshape(shape)
            w_ref[part, x] = total
            if x + 1 < nx:
                u, flux_low = u_next, flux
        if after:
            after(g)
        return carry

    lax.fori_loop(0, samples // BLOCK, body, 0)


def edge_kernel(lined, w_in, u_ref, *refs):
    del w_in
    cx0, cx1, cy0, cy1, hx0, hx1, hy0, hy1 = refs[:8]
    w_ref, lx, ux, ly, uy, *lines = refs[-7:]
    samples, nx, ny, nz = u_ref.shape
    w_rows, u_rows = flat(w_ref), flat(u_ref)

    def one(s):
        for x, coef, halo in ((0, cx0, hx0), (nx - 1, cx1, hx1)):
            w_ref[s, x] = w_ref[s, x] + coef[s] * (halo[s].astype(F32) - u_ref[s, x])
        for end, (coef, halo, out) in enumerate(((cy0, hy0, ly), (cy1, hy1, uy))):
            line = y_line(u_ref, s, end * (ny - 1))
            state = refs[8 + end][s] if lined else u_rows[line, :]
            value = w_rows[line, :] + coef[s] * (halo[s].astype(F32) - state)
            w_rows[line, :] = value
            out[s] = value.astype(BF)
            lines[end][s] = value
        lx[s] = w_ref[s, 0].astype(BF)
        ux[s] = w_ref[s, nx - 1].astype(BF)

    def body(i, carry):
        for j in range(16):
            one(i * 16 + j)
        return carry

    lax.fori_loop(0, samples // 16, body, 0)


def split_shape(shape):
    count, nx, ny, nz = shape
    return (nx, ny // ROWS, count * ROWS, nz)


def split_into(out_ref, x, value):
    count, ny, nz = value.shape
    for h in range(ny // ROWS):
        part = value[:, h * ROWS : (h + 1) * ROWS]
        out_ref[x, h] = part.reshape(count * ROWS, nz).astype(BF)


def one_hot(rows, cols, row_width, col_width):
    row = lax.broadcasted_iota(jnp.int32, (rows, cols), 0) // row_width
    col = lax.broadcasted_iota(jnp.int32, (rows, cols), 1) // col_width
    return (row == col).astype(BF)


def spread(block):
    rows, cols = block.shape
    tall = jnp.dot(one_hot(rows * ROWS, rows, ROWS, 1), block, preferred_element_type=F32).astype(BF)
    full = jnp.dot(tall, one_hot(cols, cols * ROWS, 1, ROWS), preferred_element_type=F32)
    row = lax.broadcasted_iota(jnp.int32, full.shape, 0) % ROWS
    col = lax.broadcasted_iota(jnp.int32, full.shape, 1) % ROWS
    return jnp.where(row == col, full, 0.0).astype(BF)


def lines_kernel(psi_hbm, prev_hbm, omega_ref, after, x_ref, weight_ref, prev_ref, xbuf, wide, sem):
    del after
    ranks, nx, ny, nz = psi_hbm.shape
    rows = wide.reshape(ranks * ny, nz)
    copies = []
    for end in range(2):
        copies.append(
            pltpu.make_async_copy(psi_hbm.at[:, end * (nx - 1)], xbuf.at[end], sem.at[end])
        )
    copies.append(pltpu.make_async_copy(prev_hbm, prev_ref, sem.at[2]))
    for copy in copies:
        copy.start()
    for i in range(omega_ref.shape[0]):
        weight_ref[i] = spread(omega_ref[i])
    for end in range(2):
        copies[end].wait()
        wide[...] = xbuf[end].astype(F32)
        for y in range(ny):
            x_ref[end, y] = rows[pl.ds(y, ranks, stride=ny), :].astype(BF)
    copies[2].wait()


def psi_kernel(psi_hbm, out_ref, y_ref, buf, wide, sem):
    ranks, nx, ny, nz = psi_hbm.shape
    parts = 4
    rows = wide.reshape(ranks * ny, nz)

    def copy_of(i):
        part = pl.ds(i * (nx // parts), nx // parts)
        return pltpu.make_async_copy(psi_hbm.at[:, part], buf.at[:, part], sem.at[i])

    for i in range(parts):
        copy_of(i).start()

    def body(x, carry):
        value = buf[:, x].astype(F32)
        split_into(out_ref, x, value)
        wide[...] = value
        for end in range(2):
            y_ref[end, x] = rows[pl.ds(end * (ny - 1), ranks, stride=ny), :].astype(BF)
        return carry

    for i in range(parts):
        copy_of(i).wait()
        lax.fori_loop(i * (nx // parts), (i + 1) * (nx // parts), body, 0)


def side_by_side(ref, x):
    return jnp.concatenate([ref[x, h] for h in range(ref.shape[1])], axis=1)


def range_kernel(
    weight_ref, own_ref, other_ref, prev_ref, u_ref, state_in, out_ref, state_hbm, done_ref, buf, sem
):
    del state_in
    ranks, nx, ny, nz = prev_ref.shape
    parts = 4
    inner = pl.ds(1, nx - 2)
    copies = []
    for i, (x, y) in enumerate(((0, 0), (nx - 1, ny - 1))):
        copies.append(pltpu.make_async_copy(u_ref.at[:, x], state_hbm.at[:, x], sem.at[1, i]))
        copies.append(
            pltpu.make_async_copy(u_ref.at[:, inner, y], state_hbm.at[:, inner, y], sem.at[1, 2 + i])
        )
    for copy in copies:
        copy.start()
    done_ref[...] = jnp.zeros_like(done_ref)

    def copy_of(i):
        part = pl.ds(i * (nx // parts), nx // parts)
        return pltpu.make_async_copy(buf.at[:, part], out_ref.at[:, part], sem.at[0, i])

    for i in range(parts):
        for x in range(i * (nx // parts), (i + 1) * (nx // parts)):
            value = jnp.dot(weight_ref[0], side_by_side(own_ref, x), preferred_element_type=F32)
            value += jnp.dot(weight_ref[1], side_by_side(other_ref, x), preferred_element_type=F32)
            halves = [
                value[:, h * nz : (h + 1) * nz].reshape(ranks, ROWS, nz) for h in range(ny // ROWS)
            ]
            total = jnp.concatenate(halves, axis=1) + prev_ref[:, x].astype(F32)
            buf[:, x] = total.astype(BF)
        copy_of(i).start()
    for i in range(parts):
        copy_of(i).wait()
    for copy in copies:
        copy.wait()


def corange_kernel(psi_ref, u_ref, state_in, out_ref, state_hbm, snap, acc, sem):
    del state_in
    samples, nx, ny, nz = u_ref.shape
    part = pl.ds(samples // 2, samples // 2)
    copy = pltpu.make_async_copy(u_ref.at[part], state_hbm.at[part], sem)
    copy.start()
    ranks = psi_ref.shape[2] // ROWS
    cols = ranks * ROWS
    for x in range(0, nx, 2):
        split_into(snap, x, u_ref[:, x])
        split_into(snap, x + 1, u_ref[:, x + 1])
        left = jnp.concatenate([side_by_side(snap, x), side_by_side(snap, x + 1)], axis=1)
        right = jnp.concatenate([side_by_side(psi_ref, x), side_by_side(psi_ref, x + 1)], axis=1)
        part = contract(left, right)
        acc[...] = part if x == 0 else acc[...] + part
    row = lax.broadcasted_iota(jnp.int32, (ROWS, cols), 0)
    col = lax.broadcasted_iota(jnp.int32, (ROWS, cols), 1) % ROWS
    fold = (
        lax.broadcasted_iota(jnp.int32, (cols, ranks), 0) // ROWS
        == lax.broadcasted_iota(jnp.int32, (cols, ranks), 1)
    ).astype(F32)
    picked = jnp.where((row == col)[None], acc[...].reshape(samples, ROWS, cols), 0.0).sum(1)
    out_ref[...] = jnp.dot(picked, fold, precision=lax.Precision.HIGHEST, preferred_element_type=F32)
    copy.wait()


def contract(left, right):
    return lax.dot_general(left, right, (((1,), (1,)), ((), ())), preferred_element_type=F32)


def finish_kernel(w_in, u_ref, cx0, cx1, cy0, cy1, hx0, hx1, hy0, hy1, *refs):
    del w_in
    ends, (main_ref, px, py) = refs[:2], refs[2:5]
    w_ref, out_ref, xbuf, ybuf = refs[-4:]
    samples, nx, ny, nz = u_ref.shape
    w_rows = flat(w_ref)

    def one(s):
        for end, (coef, halo) in enumerate(((cx0, hx0), (cx1, hx1))):
            x = end * (nx - 1)
            flux = coef[s] * (halo[s].astype(F32) - u_ref[s, x])
            xbuf[end, s] = flux
            w_ref[s, x] = w_ref[s, x] + flux
        for end, (coef, halo) in enumerate(((cy0, hy0), (cy1, hy1))):
            line = y_line(u_ref, s, end * (ny - 1))
            flux = coef[s] * (halo[s].astype(F32) - ends[end][s])
            ybuf[end, s] = flux
            w_rows[line, :] = w_rows[line, :] + flux

    def patch(i, carry):
        for j in range(16):
            one(i * 16 + j)
        return carry

    lax.fori_loop(0, samples // 16, patch, 0)
    total = main_ref[...]
    for buf, psi in ((xbuf, px), (ybuf, py)):
        count = buf.shape[2]
        lines = buf.reshape(2 * samples * count, nz)
        for i in range(count):
            left = [
                lines[pl.ds(end * samples * count + i, samples, stride=count), :].astype(BF)
                for end in range(2)
            ]
            right = [psi[end, i] for end in range(2)]
            total = total + contract(jnp.concatenate(left, axis=1), jnp.concatenate(right, axis=1))
    out_ref[...] = total


def snapshot_kernel(u_ref, *refs):
    snap_ref = refs[-1]

    def body(x, carry):
        split_into(snap_ref, x, u_ref[:, x])
        return carry

    lax.fori_loop(0, u_ref.shape[1], body, 0)


def sum_kernel(*refs):
    total = refs[0][...]
    for ref in refs[1:-1]:
        total = total + ref[...]
    refs[-1][...] = total


def swap_pairs(count, parity, par):
    partner = {}
    for i in range(parity, count - 1, 2):
        partner[i] = i + 1
        partner[i + 1] = i
    pairs = []
    for i in range(count):
        for p in range(par):
            source = i * par + p
            if i in partner:
                pairs.append((source, partner[i] * par + p))
            else:
                pairs.append((source, i * par + (p + 1) % par))
    return pairs


ORDER = (("sy", 0), ("sy", 1), ("sx", 0), ("sx", 1))


def exchange(faces):
    ends = {"sx": faces[:2], "sy": faces[2:]}
    par = lax.axis_size("par")
    got = {}
    for axis, parity in ORDER:
        low, high = ends[axis]
        odd = lax.axis_index(axis) % 2 == 1
        mine = jnp.where(odd, high, low) if parity else jnp.where(odd, low, high)
        pairs = swap_pairs(lax.axis_size(axis), parity, par)
        got[axis, parity] = lax.ppermute(mine, (axis, "par"), pairs)
    halos = []
    for axis in ("sx", "sy"):
        index, count = lax.axis_index(axis), lax.axis_size(axis)
        odd = index % 2 == 1
        first, second = got[axis, 0], got[axis, 1]
        zero = jnp.zeros_like(first)
        halos.append(jnp.where(index == 0, zero, jnp.where(odd, first, second)))
        halos.append(jnp.where(index == count - 1, zero, jnp.where(odd, second, first)))
    return halos


def received(value, axis):
    count = lax.axis_size(axis)
    return [lax.ppermute(value, axis, [(i, i ^ shift) for i in range(count)]) for shift in range(1, count)]


def per_device(initial_state, conductivity, omega, psi, range_prev, corange_prev):
    samples, nx, ny, nz = block = initial_state.shape
    ranks = psi.shape[0]
    cells = samples * nx * ny * nz
    x_face, y_face = (samples, ny, nz), (samples, nx, nz)
    par = lax.axis_index("par")
    par_size = lax.axis_size("par")

    sent = vmem_call(
        faces_kernel,
        [((2,) + x_face, BF)] * 2 + [((2,) + y_face, BF)] * 2,
        "faces",
        scratch=[
            pltpu.VMEM((4,) + x_face, F32),
            pltpu.VMEM((4,) + y_face, F32),
            pltpu.SemaphoreType.DMA((8,)),
        ],
        hbm_in=(0, 1),
        flops=cells // 2,
        nbytes=cells,
    )(initial_state, conductivity)
    got = exchange(sent)
    halos = [g[1] for g in got]

    groups = samples // BLOCK
    state, moved, *made = vmem_call(
        first_kernel,
        [(block, F32)] * 6 + [(x_face, F32)] * 2 + [(y_face, F32)] * 2,
        "first",
        limit=7 << 20,
        scratch=[pltpu.VMEM(block, F32), pltpu.SemaphoreType.DMA((2, groups))],
        hbm_in=(0, 1),
        flops=36 * cells,
        nbytes=16 * cells,
    )(initial_state, conductivity)
    coefs, kfaces = made[:4], made[4:]
    face_coefs = [k + HALF * g[0].astype(F32) for k, g in zip(kfaces, got)]

    own_ranks = range_prev.shape[0]
    own_cols = lax.dynamic_slice_in_dim(omega, par * own_ranks, own_ranks, 1).T
    source = (par + par_size - 1) % par_size
    omega_blocks = jnp.stack(
        [lax.dynamic_slice_in_dim(own_cols, p * samples, samples, 1) for p in (par, source)]
    )
    held_psi, psi_y = vmem_call(
        psi_kernel,
        [(split_shape(psi.shape), BF), ((2, nx, ranks, nz), BF)],
        "psi",
        limit=6 << 20,
        scratch=[
            pltpu.VMEM(psi.shape, BF),
            pltpu.VMEM((ranks, ny, nz), F32),
            pltpu.SemaphoreType.DMA((4,)),
        ],
        hbm_in=(0,),
        flops=4 * cells,
        nbytes=4 * cells,
    )(psi)
    kept = (held_psi, psi_y)
    lines = []
    for step in range(STEPS):
        if step > 0:
            halos = exchange(edges)
            last = step == STEPS - 1
            moved, *written = vmem_call(
                last_step_kernel if last else step_kernel,
                [(block, F32)] * (2 if last else 1),
                "step",
                scratch=[pltpu.SemaphoreType.DMA((groups,))] if last else [],
                hbm_out=(1,),
                flops=24 * cells,
                nbytes=8 * cells,
            )(state, *coefs, *kept)
        if step == 2:
            psi_x, weights, prev = vmem_call(
                lines_kernel,
                [
                    ((2, ny, ranks, nz), BF),
                    ((2, own_ranks * ROWS, samples * ROWS), BF),
                    (range_prev.shape, BF),
                ],
                "lines",
                limit=4 << 20,
                scratch=[
                    pltpu.VMEM((2, ranks, ny, nz), BF),
                    pltpu.VMEM((ranks, ny, nz), F32),
                    pltpu.SemaphoreType.DMA((3,)),
                ],
                hbm_in=(0, 1),
                flops=cells,
                nbytes=cells,
            )(psi, range_prev, omega_blocks, moved)
            kept += (psi_x, weights, prev)
        if step < STEPS - 1:
            outs = [(block, F32)] + [(x_face, BF)] * 2 + [(y_face, BF)] * 2 + [(y_face, F32)] * 2
            state, *edges = vmem_call(
                functools.partial(edge_kernel, step > 0),
                outs,
                "edge",
                aliases={0: 0},
                flops=cells,
                nbytes=cells,
            )(moved, state, *face_coefs, *halos, *lines, *kept)
            edges, lines = edges[:4], edges[4:]

    main, written = vmem_call(
        corange_kernel,
        [((samples, ranks), F32), (block, F32)],
        "corange",
        limit=6 << 20,
        scratch=[
            pltpu.VMEM(split_shape(block), BF),
            pltpu.VMEM((samples * ROWS, ranks * ROWS), F32),
            pltpu.SemaphoreType.DMA,
        ],
        hbm_in=(2,),
        hbm_out=(1,),
        aliases={2: 1},
        flops=2 * ranks * ROWS * cells,
        nbytes=4 * cells,
    )(held_psi, moved, *written)
    final, partial_sum = vmem_call(
        finish_kernel,
        [(block, F32), ((samples, ranks), F32)],
        "finish",
        scratch=[pltpu.VMEM((2,) + x_face, F32), pltpu.VMEM((2,) + y_face, F32)],
        aliases={0: 0},
        flops=cells,
        nbytes=2 * cells,
    )(moved, state, *face_coefs, *halos, *lines, main, psi_x, psi_y, prev, weights)
    first_sums = received(partial_sum, "sx")
    line_sum = vmem_call(
        sum_kernel, [((samples, ranks), F32)], "line_sum", flops=SUM_COST, nbytes=SUM_COST
    )(partial_sum, *first_sums)[0]
    snapshot = vmem_call(
        snapshot_kernel, [(split_shape(block), BF)], "snapshot", flops=cells, nbytes=2 * cells
    )(final, prev, weights)[0]
    other = lax.ppermute(snapshot, "par", [(i, (i + 1) % par_size) for i in range(par_size)])
    range_sketch, final_state, done = vmem_call(
        range_kernel,
        [(range_prev.shape, BF), (block, F32), ((samples, ranks), F32)],
        "range",
        limit=6 << 20,
        scratch=[pltpu.VMEM(range_prev.shape, BF), pltpu.SemaphoreType.DMA((2, 4))],
        hbm_in=(5,),
        hbm_out=(0, 1),
        aliases={5: 1},
        flops=2 * ranks * ROWS * cells,
        nbytes=4 * cells,
    )(weights, snapshot, other, prev, final, written)
    corange = sum(received(line_sum, "sy"), corange_prev.T + line_sum) + done
    return final_state, range_sketch, corange.T


def solution(mesh):
    in_specs = (
        P("par", "sx", "sy", None),
        P("par", "sx", "sy", None),
        P(),
        P(None, "sx", "sy", None),
        P("par", "sx", "sy", None),
        P(None, "par"),
    )
    out_specs = (P("par", "sx", "sy", None), P("par", "sx", "sy", None), P(None, "par"))
    return jax.shard_map(
        per_device, mesh=mesh, in_specs=in_specs, out_specs=out_specs, check_vma=False
    )
```

```python
import functools

import jax
import jax.numpy as jnp
from jax import lax
from jax.experimental import pallas as pl
from jax.experimental.pallas import tpu as pltpu
from jax.sharding import PartitionSpec as P

STEPS = 4
BF = jnp.bfloat16
F32 = jnp.float32
HALF = 0.16 * 0.5
BLOCK = 8
ROWS = 8
SUM_COST = 20 << 20


def vmem_call(
    kernel, outs, name, limit=3 << 20, scratch=(), hbm_in=(), hbm_out=(), aliases=None, flops=0, nbytes=0
):
    def call(*args):
        in_specs = []
        ready = []
        for i, arg in enumerate(args):
            in_specs.append(pl.BlockSpec(memory_space=pltpu.HBM if i in hbm_in else pltpu.VMEM))
            ready.append(
                pltpu.with_memory_space_constraint(arg, pltpu.HBM if i in hbm_in else pltpu.VMEM)
            )
        out_shape = []
        out_specs = []
        for i, (shape, dtype) in enumerate(outs):
            out_shape.append((pltpu.HBM if i in hbm_out else pltpu.VMEM)(shape, dtype))
            out_specs.append(pl.BlockSpec(memory_space=pltpu.HBM if i in hbm_out else pltpu.VMEM))
        return pl.pallas_call(
            kernel,
            out_shape=out_shape,
            in_specs=in_specs,
            out_specs=out_specs,
            scratch_shapes=list(scratch),
            input_output_aliases=aliases or {},
            name=name,
            compiler_params=pltpu.CompilerParams(vmem_limit_bytes=limit),
            cost_estimate=pl.CostEstimate(flops=flops, bytes_accessed=nbytes, transcendentals=0),
        )(*ready)

    return call


def faces_kernel(u_ref, k_ref, lx, ux, ly, uy, xbuf, ybuf, sem):
    _, nx, ny, _ = u_ref.shape
    copies = []
    for i, (ref, end) in enumerate(((k_ref, 0), (u_ref, 0), (k_ref, 1), (u_ref, 1))):
        x, y = end * (nx - 1), end * (ny - 1)
        copies.append(pltpu.make_async_copy(ref.at[:, x], xbuf.at[i], sem.at[i]))
        copies.append(pltpu.make_async_copy(ref.at[:, :, y], ybuf.at[i], sem.at[4 + i]))
    for copy in copies:
        copy.start()
    for i in range(4):
        copies[2 * i].wait()
        copies[2 * i + 1].wait()
        (lx if i < 2 else ux)[i % 2] = xbuf[i].astype(BF)
        (ly if i < 2 else uy)[i % 2] = ybuf[i].astype(BF)


def y_line(ref, s, y):
    _, nx, ny, _ = ref.shape
    return pl.ds(s * (nx * ny) + y, nx, stride=ny)


def flat(ref):
    samples, nx, ny, nz = ref.shape
    return ref.reshape(samples * nx * ny, nz)


def first_kernel(
    u_hbm, k_hbm, u_ref, w_ref, cx_ref, cy_ref, cup_ref, cdown_ref, kx0, kx1, ky0, ky1, buf, sem
):
    samples, nx, ny, nz = u_ref.shape
    shape = (BLOCK, ny, nz)
    groups = samples // BLOCK
    y_open = lax.broadcasted_iota(jnp.int32, shape, 1) < ny - 1
    lane = lax.broadcasted_iota(jnp.int32, shape, 2)
    rows = flat(buf)

    def copies(g):
        part = pl.ds(g * BLOCK, BLOCK)
        return (
            pltpu.make_async_copy(k_hbm.at[part], buf.at[part], sem.at[0, g]),
            pltpu.make_async_copy(u_hbm.at[part], u_ref.at[part], sem.at[1, g]),
        )

    for g in range(groups):
        for copy in copies(g):
            copy.start()

    def before(g):
        for copy in copies(g):
            copy.wait()
        part = pl.ds(g * BLOCK, BLOCK)
        for i in range(BLOCK):
            s = g * BLOCK + i
            ky0[s] = rows[y_line(buf, s, 0), :] * HALF
            ky1[s] = rows[y_line(buf, s, ny - 1), :] * HALF
        k = buf[part, 0] * HALF
        kx0[part] = k
        for x in range(nx):
            if x + 1 < nx:
                k_next = buf[part, x + 1] * HALF
                cx_ref[part, x] = k + k_next
            cy_ref[part, x] = jnp.where(y_open, k + pltpu.roll(k, ny - 1, 1), 0.0)
            cup_ref[part, x] = k + jnp.where(lane < nz - 1, pltpu.roll(k, nz - 1, 2), 0.0)
            cdown_ref[part, x] = k + jnp.where(lane > 0, pltpu.roll(k, 1, 2), 0.0)
            if x + 1 < nx:
                k = k_next
        kx1[part] = k

    step_body(u_ref, cx_ref, cy_ref, cup_ref, cdown_ref, w_ref, before)


def difference_matrix(nz):
    row = lax.broadcasted_iota(jnp.int32, (nz, nz), 0)
    col = lax.broadcasted_iota(jnp.int32, (nz, nz), 1)
    eye = (row == col).astype(F32)
    up = (row == col + 1).astype(F32) - eye
    down = (row + 1 == col).astype(F32) - eye
    both = jnp.concatenate([up, down], axis=1).astype(BF)
    return jnp.concatenate([both, both], axis=0)


def step_kernel(u_ref, cx_ref, cy_ref, cup_ref, cdown_ref, *refs):
    step_body(u_ref, cx_ref, cy_ref, cup_ref, cdown_ref, refs[-1])


def last_step_kernel(u_ref, cx_ref, cy_ref, cup_ref, cdown_ref, *refs):
    w_ref, state_hbm, sem = refs[-3:]
    half = u_ref.shape[0] // BLOCK // 2

    def copy_of(g):
        part = pl.ds(g * BLOCK, BLOCK)
        return pltpu.make_async_copy(w_ref.at[part], state_hbm.at[part], sem.at[g])

    def after(g):
        @pl.when(g < half)
        def _():
            copy_of(g).start()

    step_body(u_ref, cx_ref, cy_ref, cup_ref, cdown_ref, w_ref, after=after)
    for g in range(half):
        copy_of(g).wait()


def step_body(u_ref, cx_ref, cy_ref, cup_ref, cdown_ref, w_ref, before=None, after=None):
    samples, nx, ny, nz = u_ref.shape
    shape = (BLOCK, ny, nz)
    matrix = difference_matrix(nz)

    def body(g, carry):
        if before:
            before(g)
        part = pl.ds(g * BLOCK, BLOCK)
        u = u_ref[part, 0]
        for x in range(nx):
            total = u
            if x + 1 < nx:
                u_next = u_ref[part, x + 1]
                flux = cx_ref[part, x] * (u_next - u)
                total = total + flux
            if x > 0:
                total = total - flux_low
            fy = cy_ref[part, x] * (pltpu.roll(u, ny - 1, 1) - u)
            total = total + (fy - pltpu.roll(fy, 1, 1))
            wide = u.reshape(BLOCK * ny, nz)
            coarse = wide.astype(BF)
            fine = (wide - coarse.astype(F32)).astype(BF)
            dz = jnp.dot(jnp.concatenate([coarse, fine], axis=1), matrix, preferred_element_type=F32)
            total = total + cup_ref[part, x] * dz[:, :nz].reshape(shape)
            total = total + cdown_ref[part, x] * dz[:, nz:].reshape(shape)
            w_ref[part, x] = total
            if x + 1 < nx:
                u, flux_low = u_next, flux
        if after:
            after(g)
        return carry

    lax.fori_loop(0, samples // BLOCK, body, 0)


def edge_kernel(first, w_in, u_ref, *refs):
    del w_in
    coefs, halos = refs[:4], refs[4:8]
    made = refs[-4:] if first else ()
    w_ref, lx, ux, ly, uy, *lines = refs[-11:-4] if first else refs[-7:]
    samples, nx, ny, nz = u_ref.shape
    w_rows, u_rows = flat(w_ref), flat(u_ref)

    def flux(i, s, state):
        if first:
            coef = coefs[i][s] + HALF * halos[i][0, s].astype(F32)
            made[i][s] = coef
            return coef * (halos[i][1, s].astype(F32) - state)
        return coefs[i][s] * (halos[i][s].astype(F32) - state)

    def one(s):
        for i, x in enumerate((0, nx - 1)):
            w_ref[s, x] = w_ref[s, x] + flux(i, s, u_ref[s, x])
        for end, out in enumerate((ly, uy)):
            line = y_line(u_ref, s, end * (ny - 1))
            state = u_rows[line, :] if first else refs[8 + end][s]
            value = w_rows[line, :] + flux(2 + end, s, state)
            w_rows[line, :] = value
            out[s] = value.astype(BF)
            lines[end][s] = value
        lx[s] = w_ref[s, 0].astype(BF)
        ux[s] = w_ref[s, nx - 1].astype(BF)

    def body(i, carry):
        for j in range(16):
            one(i * 16 + j)
        return carry

    lax.fori_loop(0, samples // 16, body, 0)


def split_shape(shape):
    count, nx, ny, nz = shape
    return (nx, ny // ROWS, count * ROWS, nz)


def split_into(out_ref, x, value):
    count, ny, nz = value.shape
    for h in range(ny // ROWS):
        part = value[:, h * ROWS : (h + 1) * ROWS]
        out_ref[x, h] = part.reshape(count * ROWS, nz).astype(BF)


def spread(omega, ranks, samples, rank_group, sample_group):
    rows, cols = ranks * ROWS, samples * ROWS

    def pick(count, axis, group, width):
        shape = (count, omega.shape[axis])
        row = lax.broadcasted_iota(jnp.int32, shape, 0) // ROWS + group * width
        return (row == lax.broadcasted_iota(jnp.int32, shape, 1)).astype(BF)

    tall = contract(pick(rows, 1, rank_group, ranks), omega).astype(BF)
    full = contract(tall, pick(cols, 0, sample_group, samples))
    row = lax.broadcasted_iota(jnp.int32, full.shape, 0) % ROWS
    col = lax.broadcasted_iota(jnp.int32, full.shape, 1) % ROWS
    return jnp.where(row == col, full, 0.0).astype(BF)


def lines_kernel(psi_hbm, prev_hbm, omega_ref, after, x_ref, weight_ref, prev_ref, xbuf, wide, sem):
    del after
    ranks, nx, ny, nz = psi_hbm.shape
    rows = wide.reshape(ranks * ny, nz)
    copies = []
    for end in range(2):
        copies.append(
            pltpu.make_async_copy(psi_hbm.at[:, end * (nx - 1)], xbuf.at[end], sem.at[end])
        )
    copies.append(pltpu.make_async_copy(prev_hbm, prev_ref, sem.at[2]))
    for copy in copies:
        copy.start()
    group, groups = lax.axis_index("par"), lax.axis_size("par")
    for i in range(2):
        source = (group + i * (groups - 1)) % groups
        shape = [n // ROWS for n in weight_ref.shape[1:]]
        weight_ref[i] = spread(omega_ref[...], *shape, group, source)
    for end in range(2):
        copies[end].wait()
        wide[...] = xbuf[end].astype(F32)
        for y in range(ny):
            x_ref[end, y] = rows[pl.ds(y, ranks, stride=ny), :].astype(BF)
    copies[2].wait()


def psi_kernel(psi_hbm, out_ref, y_ref, buf, wide, sem):
    ranks, nx, ny, nz = psi_hbm.shape
    parts = 4
    rows = wide.reshape(ranks * ny, nz)

    def copy_of(i):
        part = pl.ds(i * (nx // parts), nx // parts)
        return pltpu.make_async_copy(psi_hbm.at[:, part], buf.at[:, part], sem.at[i])

    for i in range(parts):
        copy_of(i).start()

    def body(x, carry):
        value = buf[:, x].astype(F32)
        split_into(out_ref, x, value)
        wide[...] = value
        for end in range(2):
            y_ref[end, x] = rows[pl.ds(end * (ny - 1), ranks, stride=ny), :].astype(BF)
        return carry

    for i in range(parts):
        copy_of(i).wait()
        lax.fori_loop(i * (nx // parts), (i + 1) * (nx // parts), body, 0)


def side_by_side(ref, x):
    return jnp.concatenate([ref[x, h] for h in range(ref.shape[1])], axis=1)


def range_kernel(
    weight_ref, own_ref, other_ref, prev_ref, u_ref, state_in, out_ref, state_hbm, done_ref, buf, sem
):
    del state_in
    ranks, nx, ny, nz = prev_ref.shape
    parts = 4
    inner = pl.ds(1, nx - 2)
    copies = []
    for i, (x, y) in enumerate(((0, 0), (nx - 1, ny - 1))):
        copies.append(pltpu.make_async_copy(u_ref.at[:, x], state_hbm.at[:, x], sem.at[1, i]))
        copies.append(
            pltpu.make_async_copy(u_ref.at[:, inner, y], state_hbm.at[:, inner, y], sem.at[1, 2 + i])
        )
    for copy in copies:
        copy.start()
    done_ref[...] = jnp.zeros_like(done_ref)

    def copy_of(i):
        part = pl.ds(i * (nx // parts), nx // parts)
        return pltpu.make_async_copy(buf.at[:, part], out_ref.at[:, part], sem.at[0, i])

    for i in range(parts):
        for x in range(i * (nx // parts), (i + 1) * (nx // parts)):
            value = jnp.dot(weight_ref[0], side_by_side(own_ref, x), preferred_element_type=F32)
            value += jnp.dot(weight_ref[1], side_by_side(other_ref, x), preferred_element_type=F32)
            halves = [
                value[:, h * nz : (h + 1) * nz].reshape(ranks, ROWS, nz) for h in range(ny // ROWS)
            ]
            total = jnp.concatenate(halves, axis=1) + prev_ref[:, x].astype(F32)
            buf[:, x] = total.astype(BF)
        copy_of(i).start()
    for i in range(parts):
        copy_of(i).wait()
    for copy in copies:
        copy.wait()


def corange_kernel(psi_ref, u_ref, state_in, out_ref, state_hbm, snap, acc, sem):
    del state_in
    samples, nx, ny, nz = u_ref.shape
    part = pl.ds(samples // 2, samples // 2)
    copy = pltpu.make_async_copy(u_ref.at[part], state_hbm.at[part], sem)
    copy.start()
    ranks = psi_ref.shape[2] // ROWS
    cols = ranks * ROWS
    for x in range(0, nx, 2):
        split_into(snap, x, u_ref[:, x])
        split_into(snap, x + 1, u_ref[:, x + 1])
        left = jnp.concatenate([side_by_side(snap, x), side_by_side(snap, x + 1)], axis=1)
        right = jnp.concatenate([side_by_side(psi_ref, x), side_by_side(psi_ref, x + 1)], axis=1)
        part = contract(left, right)
        acc[...] = part if x == 0 else acc[...] + part
    row = lax.broadcasted_iota(jnp.int32, (ROWS, cols), 0)
    col = lax.broadcasted_iota(jnp.int32, (ROWS, cols), 1) % ROWS
    fold = (
        lax.broadcasted_iota(jnp.int32, (cols, ranks), 0) // ROWS
        == lax.broadcasted_iota(jnp.int32, (cols, ranks), 1)
    ).astype(F32)
    picked = jnp.where((row == col)[None], acc[...].reshape(samples, ROWS, cols), 0.0).sum(1)
    out_ref[...] = jnp.dot(picked, fold, precision=lax.Precision.HIGHEST, preferred_element_type=F32)
    copy.wait()


def contract(left, right):
    return lax.dot_general(left, right, (((1,), (1,)), ((), ())), preferred_element_type=F32)


def finish_kernel(w_in, u_ref, cx0, cx1, cy0, cy1, hx0, hx1, hy0, hy1, *refs):
    del w_in
    ends, (main_ref, px, py) = refs[:2], refs[2:5]
    w_ref, out_ref, xbuf, ybuf = refs[-4:]
    samples, nx, ny, nz = u_ref.shape
    w_rows = flat(w_ref)

    def one(s):
        for end, (coef, halo) in enumerate(((cx0, hx0), (cx1, hx1))):
            x = end * (nx - 1)
            flux = coef[s] * (halo[s].astype(F32) - u_ref[s, x])
            xbuf[end, s] = flux
            w_ref[s, x] = w_ref[s, x] + flux
        for end, (coef, halo) in enumerate(((cy0, hy0), (cy1, hy1))):
            line = y_line(u_ref, s, end * (ny - 1))
            flux = coef[s] * (halo[s].astype(F32) - ends[end][s])
            ybuf[end, s] = flux
            w_rows[line, :] = w_rows[line, :] + flux

    def patch(i, carry):
        for j in range(16):
            one(i * 16 + j)
        return carry

    lax.fori_loop(0, samples // 16, patch, 0)
    total = main_ref[...]
    for buf, psi in ((xbuf, px), (ybuf, py)):
        count = buf.shape[2]
        lines = buf.reshape(2 * samples * count, nz)
        for i in range(count):
            left = [
                lines[pl.ds(end * samples * count + i, samples, stride=count), :].astype(BF)
                for end in range(2)
            ]
            right = [psi[end, i] for end in range(2)]
            total = total + contract(jnp.concatenate(left, axis=1), jnp.concatenate(right, axis=1))
    out_ref[...] = total


def snapshot_kernel(u_ref, *refs):
    snap_ref = refs[-1]

    def body(x, carry):
        split_into(snap_ref, x, u_ref[:, x])
        return carry

    lax.fori_loop(0, u_ref.shape[1], body, 0)


def sum_kernel(*refs):
    total = refs[0][...]
    for ref in refs[1:-1]:
        total = total + ref[...]
    refs[-1][...] = total


def swap_pairs(count, parity, par):
    partner = {}
    for i in range(parity, count - 1, 2):
        partner[i] = i + 1
        partner[i + 1] = i
    pairs = []
    for i in range(count):
        for p in range(par):
            source = i * par + p
            if i in partner:
                pairs.append((source, partner[i] * par + p))
            else:
                pairs.append((source, i * par + (p + 1) % par))
    return pairs


ORDER = (("sy", 0), ("sy", 1), ("sx", 0), ("sx", 1))


def exchange(faces):
    ends = {"sx": faces[:2], "sy": faces[2:]}
    par = lax.axis_size("par")
    got = {}
    for axis, parity in ORDER:
        low, high = ends[axis]
        odd = lax.axis_index(axis) % 2 == 1
        mine = jnp.where(odd, high, low) if parity else jnp.where(odd, low, high)
        pairs = swap_pairs(lax.axis_size(axis), parity, par)
        got[axis, parity] = lax.ppermute(mine, (axis, "par"), pairs)
    halos = []
    for axis in ("sx", "sy"):
        index, count = lax.axis_index(axis), lax.axis_size(axis)
        odd = index % 2 == 1
        first, second = got[axis, 0], got[axis, 1]
        zero = jnp.zeros_like(first)
        halos.append(jnp.where(index == 0, zero, jnp.where(odd, first, second)))
        halos.append(jnp.where(index == count - 1, zero, jnp.where(odd, second, first)))
    return halos


def received(value, axis):
    count = lax.axis_size(axis)
    return [lax.ppermute(value, axis, [(i, i ^ shift) for i in range(count)]) for shift in range(1, count)]


def per_device(initial_state, conductivity, omega, psi, range_prev, corange_prev):
    samples, nx, ny, nz = block = initial_state.shape
    ranks = psi.shape[0]
    cells = samples * nx * ny * nz
    x_face, y_face = (samples, ny, nz), (samples, nx, nz)
    par = lax.axis_index("par")
    par_size = lax.axis_size("par")

    sent = vmem_call(
        faces_kernel,
        [((2,) + x_face, BF)] * 2 + [((2,) + y_face, BF)] * 2,
        "faces",
        scratch=[
            pltpu.VMEM((4,) + x_face, F32),
            pltpu.VMEM((4,) + y_face, F32),
            pltpu.SemaphoreType.DMA((8,)),
        ],
        hbm_in=(0, 1),
        flops=cells // 2,
        nbytes=cells,
    )(initial_state, conductivity)
    got = exchange(sent)
    halos = got

    groups = samples // BLOCK
    state, moved, *made = vmem_call(
        first_kernel,
        [(block, F32)] * 6 + [(x_face, F32)] * 2 + [(y_face, F32)] * 2,
        "first",
        limit=7 << 20,
        scratch=[pltpu.VMEM(block, F32), pltpu.SemaphoreType.DMA((2, groups))],
        hbm_in=(0, 1),
        flops=36 * cells,
        nbytes=16 * cells,
    )(initial_state, conductivity)
    coefs, kfaces = made[:4], made[4:]
    face_coefs = kfaces

    own_ranks = range_prev.shape[0]
    held_psi, psi_y = vmem_call(
        psi_kernel,
        [(split_shape(psi.shape), BF), ((2, nx, ranks, nz), BF)],
        "psi",
        limit=6 << 20,
        scratch=[
            pltpu.VMEM(psi.shape, BF),
            pltpu.VMEM((ranks, ny, nz), F32),
            pltpu.SemaphoreType.DMA((4,)),
        ],
        hbm_in=(0,),
        flops=4 * cells,
        nbytes=4 * cells,
    )(psi)
    kept = (held_psi, psi_y)
    lines = []
    for step in range(STEPS):
        if step > 0:
            halos = exchange(edges)
            last = step == STEPS - 1
            moved, *written = vmem_call(
                last_step_kernel if last else step_kernel,
                [(block, F32)] * (2 if last else 1),
                "step",
                scratch=[pltpu.SemaphoreType.DMA((groups,))] if last else [],
                hbm_out=(1,),
                flops=24 * cells,
                nbytes=8 * cells,
            )(state, *coefs, *kept)
        if step == 2:
            psi_x, weights, prev = vmem_call(
                lines_kernel,
                [
                    ((2, ny, ranks, nz), BF),
                    ((2, own_ranks * ROWS, samples * ROWS), BF),
                    (range_prev.shape, BF),
                ],
                "lines",
                limit=4 << 20,
                scratch=[
                    pltpu.VMEM((2, ranks, ny, nz), BF),
                    pltpu.VMEM((ranks, ny, nz), F32),
                    pltpu.SemaphoreType.DMA((3,)),
                ],
                hbm_in=(0, 1),
                flops=cells,
                nbytes=cells,
            )(psi, range_prev, omega, moved)
            kept += (psi_x, weights, prev)
        if step < STEPS - 1:
            outs = [(block, F32)] + [(x_face, BF)] * 2 + [(y_face, BF)] * 2 + [(y_face, F32)] * 2
            if step == 0:
                outs += [(x_face, F32)] * 2 + [(y_face, F32)] * 2
            state, *edges = vmem_call(
                functools.partial(edge_kernel, step == 0),
                outs,
                "edge",
                aliases={0: 0},
                flops=cells,
                nbytes=cells,
            )(moved, state, *face_coefs, *halos, *lines, *kept)
            if step == 0:
                face_coefs = edges[6:]
            edges, lines = edges[:4], edges[4:6]

    main, written = vmem_call(
        corange_kernel,
        [((samples, ranks), F32), (block, F32)],
        "corange",
        limit=6 << 20,
        scratch=[
            pltpu.VMEM(split_shape(block), BF),
            pltpu.VMEM((samples * ROWS, ranks * ROWS), F32),
            pltpu.SemaphoreType.DMA,
        ],
        hbm_in=(2,),
        hbm_out=(1,),
        aliases={2: 1},
        flops=2 * ranks * ROWS * cells,
        nbytes=4 * cells,
    )(held_psi, moved, *written)
    final, partial_sum = vmem_call(
        finish_kernel,
        [(block, F32), ((samples, ranks), F32)],
        "finish",
        scratch=[pltpu.VMEM((2,) + x_face, F32), pltpu.VMEM((2,) + y_face, F32)],
        aliases={0: 0},
        flops=cells,
        nbytes=2 * cells,
    )(moved, state, *face_coefs, *halos, *lines, main, psi_x, psi_y, prev, weights)
    first_sums = received(partial_sum, "sx")
    line_sum = vmem_call(
        sum_kernel, [((samples, ranks), F32)], "line_sum", flops=SUM_COST, nbytes=SUM_COST
    )(partial_sum, *first_sums)[0]
    snapshot = vmem_call(
        snapshot_kernel, [(split_shape(block), BF)], "snapshot", flops=cells, nbytes=2 * cells
    )(final, prev, weights)[0]
    other = lax.ppermute(snapshot, "par", [(i, (i + 1) % par_size) for i in range(par_size)])
    range_sketch, final_state, done = vmem_call(
        range_kernel,
        [(range_prev.shape, BF), (block, F32), ((samples, ranks), F32)],
        "range",
        limit=6 << 20,
        scratch=[pltpu.VMEM(range_prev.shape, BF), pltpu.SemaphoreType.DMA((2, 4))],
        hbm_in=(5,),
        hbm_out=(0, 1),
        aliases={5: 1},
        flops=2 * ranks * ROWS * cells,
        nbytes=4 * cells,
    )(weights, snapshot, other, prev, final, written)
    corange = sum(received(line_sum, "sy"), corange_prev.T + line_sum) + done
    return final_state, range_sketch, corange.T


def solution(mesh):
    in_specs = (
        P("par", "sx", "sy", None),
        P("par", "sx", "sy", None),
        P(),
        P(None, "sx", "sy", None),
        P("par", "sx", "sy", None),
        P(None, "par"),
    )
    out_specs = (P("par", "sx", "sy", None), P("par", "sx", "sy", None), P(None, "par"))
    return jax.shard_map(
        per_device, mesh=mesh, in_specs=in_specs, out_specs=out_specs, check_vma=False
    )
```
